128 devices in a mesh: dp: 8 (over z, x_lo), row: 2 (over x_hi), col: 8 (over y, core).
Axes of the slice: x: 4 (x_hi: 2, x_lo: 2; x = x_hi * 2 + x_lo), y: 4, z: 4, core: 2. Of those that a mesh axis runs over, the one named last changes fastest.
Arguments:
- inputs: bfloat16 [16512, 1024], P(('dp', 'col'), 'row'), may hold values from -6 to 6
- w_qkv: bfloat16 [1, 1024, 3072], P(None, 'row', 'col'), may hold values from -0.1875 to 0.1875
- qv_bias: bfloat16 [1, 8, 2, 1, 128], P(None, 'col', 'row'), may hold values from -0.059814453 to 0.059814453
- w_out: bfloat16 [1, 1024, 1024], P(None, 'col', 'row'), may hold values from -6 to 6
- w_fc1: bfloat16 [1, 1024, 4096], P(None, 'row', 'col'), may hold values from -0.1875 to 0.1875
- fc1_bias: bfloat16 [1, 8, 2, 256], P(None, 'col', 'row'), may hold values from -1.796875 to 1.796875
- w_fc2: bfloat16 [1, 4096, 1024], P(None, 'col', 'row'), may hold values from -0.09375 to 0.09375
- ln_gain: bfloat16 [1, 2, 1024], P(None, None, 'row'), may hold values from 0.5 to 1.5
- ln_bias: bfloat16 [1, 2, 1024], P(None, None, 'row'), may hold values from -1.1953125 to 1.1953125
- layer_scale: bfloat16 [1, 2, 1024], P(None, None, 'row'), may hold values from 0.5 to 1.5
- branch_bias: bfloat16 [1, 2, 1024], P(None, None, 'row'), may hold values from -1.1953125 to 1.1953125
- cotangent: bfloat16 [16512, 1024], P(('dp', 'col'), 'row'), may hold values from -6 to 6
Outputs:
- output: float32 [16512, 1024], P(('dp', 'col'), 'row')
- input_grad: float32 [16512, 1024], P(('dp', 'col'), 'row')
- grad_w_qkv: float32 [1, 1024, 3072], P(None, 'row', 'col')
- grad_qv_bias: float32 [1, 8, 2, 1, 128], P(None, 'col', 'row')
- grad_w_out: float32 [1, 1024, 1024], P(None, 'col', 'row')
- grad_w_fc1: float32 [1, 1024, 4096], P(None, 'row', 'col')
- grad_fc1_bias: float32 [1, 8, 2, 256], P(None, 'col', 'row')
- grad_w_fc2: float32 [1, 4096, 1024], P(None, 'col', 'row')
- grad_ln_gain: float32 [1, 2, 1024], P(None, None, 'row')
- grad_ln_bias: float32 [1, 2, 1024], P(None, None, 'row')
- grad_layer_scale: float32 [1, 2, 1024], P(None, None, 'row')
- grad_branch_bias: float32 [1, 2, 1024], P(None, None, 'row')
The draws below stay inside these ranges and needn't reach their ends.
All inputs are finite; a program needn't handle non-finite values.
Results may differ from the reference program's by a relative error of at most 0.0098.
Values may be sent and summed in bfloat16 or wider, within the bound.
No kernel may reach another device: no remote copies, remote signals or barrier semaphores. Data moves between devices by JAX's collectives and lax.ppermute only.
A program may use at most 128 MiB of HBM per device.

```python
import math
import jax
import jax.numpy as jnp
from jax import lax

D = 1024
H = 16
FF = 4096
HD = 64
LAYERS = 1
SEQ = 1025
SEQP = 1032
TOKENS = 16512
HPD = 1
FPD = 256
N_ROW = 2
N_COL = 8


def shard_levels(stream_key, extent, cuts, low, top_value):
    def one(position, blocks):
        steps = jax.random.uniform(jax.random.fold_in(jax.random.fold_in(stream_key, 6), position), (blocks,), jnp.float32, low / len(cuts), top_value / len(cuts))
        return jnp.repeat(jnp.exp(steps), extent[position] // blocks).reshape((-1,) + (1,) * (len(extent) - position - 1))

    loudness = one(*cuts[0])
    for cut in cuts[1:]:
        loudness = loudness * one(*cut)
    return loudness


def normal_values(key, extent, scale, most, split=(), kind=jnp.bfloat16):
    array = scale * jax.random.normal(key, extent, jnp.float32)
    if split:
        array = array * shard_levels(key, extent, split, -0.22, 0.18)
    return jnp.clip(array, -most, most).astype(kind)


def setup_inputs(seed: int = 0) -> dict:
    key_of = jax.random.split(jax.random.key(seed), 13)
    inputs = normal_values(key_of[0], (TOKENS, D), 1.0, 6.0, ((0, 64), (1, 2)))
    w_qkv = normal_values(key_of[1], (LAYERS, D, 3 * D), D ** -0.5, 0.1875, ((1, 2), (2, 8)))
    qv_bias = normal_values(key_of[2], (LAYERS, N_COL, N_ROW, HPD, 2 * HD), 0.01, 0.059814453, ((1, 8), (2, 2)))
    w_out = normal_values(key_of[3], (LAYERS, D, D), (max(1, D // SEQ)) ** -0.5, 6.0, ((1, 8), (2, 2)))
    w_fc1 = normal_values(key_of[4], (LAYERS, D, FF), D ** -0.5, 0.1875, ((1, 2), (2, 8)))
    fc1_bias = normal_values(key_of[5], (LAYERS, N_COL, N_ROW, FPD), 0.3, 1.796875, ((1, 8), (2, 2)))
    w_fc2 = normal_values(key_of[6], (LAYERS, FF, D), FF ** -0.5, 0.09375, ((1, 8), (2, 2)))
    ln_gain = jnp.clip(1.0 + 0.1 * jax.random.normal(key_of[7], (LAYERS, 2, D), jnp.float32), 0.5, 1.5).astype(jnp.bfloat16)
    ln_bias = normal_values(key_of[8], (LAYERS, 2, D), 0.2, 1.1953125, ((2, 2),))
    layer_scale = jnp.clip(jnp.exp(math.log(1.5) - 1.0986123 * jax.random.uniform(key_of[9], (LAYERS, 2, D), jnp.float32) ** shard_levels(key_of[9], (LAYERS, 2, D), ((2, 2),), -0.2, 0.2)), 0.5, 1.5).astype(jnp.bfloat16)
    branch_bias = normal_values(key_of[10], (LAYERS, 2, D), 0.2, 1.1953125, ((2, 2),))
    cotangent = normal_values(key_of[11], (TOKENS, D), 1.0, 6.0, ((0, 64), (1, 2)))
    return {"inputs": inputs, "w_qkv": w_qkv, "qv_bias": qv_bias, "w_out": w_out, "w_fc1": w_fc1, "fc1_bias": fc1_bias, "w_fc2": w_fc2, "ln_gain": ln_gain, "ln_bias": ln_bias, "layer_scale": layer_scale, "branch_bias": branch_bias, "cotangent": cotangent}


@jax.custom_vjp
def low(v):
    return lax.optimization_barrier(v.astype(jnp.bfloat16)).astype(jnp.float32)

@jax.custom_vjp
def low_back(v):
    return v

def low_keep(v):
    return (low(v), None)

def low_pass(kept, grad):
    return (grad,)

def back_keep(v):
    return (v, None)

def back_low(kept, grad):
    return (low(grad),)
low.defvjp(low_keep, low_pass)
low_back.defvjp(back_keep, back_low)
EPSILON = 1e-06
MASKED = -1000000000.0

def matmul(first_side, second_side):
    return jnp.dot(first_side, second_side, precision=lax.Precision.HIGHEST)

def layer_norm(values, norm_gain, norm_shift):
    center = lax.optimization_barrier(jnp.mean(values, axis=-1, keepdims=True))
    spread = lax.optimization_barrier(jnp.mean((values - center) ** 2, axis=-1, keepdims=True))
    return (values - center) * lax.rsqrt(spread + EPSILON) * norm_gain + norm_shift

def attend(image_block):
    query_rows, key_rows, value_rows = image_block
    scores = jnp.einsum('qhd,khd->hqk', query_rows, key_rows, precision=lax.Precision.HIGHEST)
    scores = low_back(scores * (1.0 / math.sqrt(HD)))
    within = jnp.arange(SEQP) < SEQ
    scores = jnp.where(within[None, None, :], scores, MASKED)
    highest = lax.optimization_barrier(jnp.max(scores, axis=-1, keepdims=True))
    weights = jnp.exp(scores - highest)
    softmax_out = weights / lax.optimization_barrier(jnp.sum(weights, axis=-1, keepdims=True))
    return jnp.einsum('hqk,khd->qhd', low(softmax_out), value_rows, precision=lax.Precision.HIGHEST)

def forward(stream, params):
    w_qkv, qv_bias, w_out, w_fc1, fc1_bias, w_fc2, ln_gain, ln_bias, layer_scale, branch_bias = params
    images = stream.shape[0] // SEQP
    for layer_index in range(LAYERS):
        normed = low(layer_norm(stream, ln_gain[layer_index, 0], ln_bias[layer_index, 0]))
        head_bias = qv_bias[layer_index].reshape(H, 2 * HD)
        query_bias = head_bias[:, :HD]
        full_bias = jnp.stack([query_bias, jnp.zeros_like(query_bias), head_bias[:, HD:]], axis=1).reshape(3 * D)
        packed = low(low_back(matmul(normed, w_qkv[layer_index]) + full_bias))
        packed = packed.reshape(images, SEQP, H, 3, HD)
        mixture = lax.map(jax.checkpoint(attend), (packed[:, :, :, 0], packed[:, :, :, 1], packed[:, :, :, 2]))
        mixture = low(low_back(mixture.reshape(images * SEQP, D)))
        branch = low_back(matmul(mixture, w_out[layer_index]) + branch_bias[layer_index, 0])
        stream = stream + layer_scale[layer_index, 0] * branch
        normed = low(layer_norm(stream, ln_gain[layer_index, 1], ln_bias[layer_index, 1]))
        hidden = low_back(matmul(normed, w_fc1[layer_index]) + fc1_bias[layer_index].reshape(FF))
        active = low(jax.nn.gelu(hidden, approximate=False))
        branch = low_back(matmul(active, w_fc2[layer_index]) + branch_bias[layer_index, 1])
        stream = stream + layer_scale[layer_index, 1] * branch
    return stream

def reference(inputs, w_qkv, qv_bias, w_out, w_fc1, fc1_bias, w_fc2, ln_gain, ln_bias, layer_scale, branch_bias, cotangent):
    params = (w_qkv.astype(jnp.float32), qv_bias.astype(jnp.float32), w_out.astype(jnp.float32), w_fc1.astype(jnp.float32), fc1_bias.astype(jnp.float32), w_fc2.astype(jnp.float32), ln_gain.astype(jnp.float32), ln_bias.astype(jnp.float32), layer_scale.astype(jnp.float32), branch_bias.astype(jnp.float32))
    output, pullback = jax.vjp(forward, inputs.astype(jnp.float32), params)
    input_grad, param_grads = pullback(cotangent.astype(jnp.float32))
    return (output, input_grad, param_grads[0], param_grads[1], param_grads[2], param_grads[3], param_grads[4], param_grads[5], param_grads[6], param_grads[7], param_grads[8], param_grads[9])
```

```python
import math

import jax
import jax.numpy as jnp
from jax import lax
from jax.sharding import Mesh, PartitionSpec as P

D = 1024
HD = 64
SEQ = 1025
EPSILON = 1e-06
MASKED = -1000000000.0

HALF = 129
ROWS = 136
SLOTS = 8
NY = 4
NZ = 4

F32 = jnp.float32
BF = jnp.bfloat16
GROUP = ("xh", "y", "c")


def is_home(r, y):
    return y // 2 == r


def group_index(r, y, c):
    return (r * NY + y % NY) * 2 + c


def entry_pairs():
    places = [(r, y, c) for r in range(2) for y in range(NY) for c in range(2)]
    first, second = [], []
    for r, y, c in places:
        me = group_index(r, y, c)
        if is_home(r, y):
            first.append((me, group_index(r, y + 2, c)))
        else:
            first.append((me, group_index(1 - r, y, c)))
            second.append((me, group_index(1 - r, y + 2, c)))
    return first, second


ENTRY_FIRST, ENTRY_SECOND = entry_pairs()
EXIT_FIRST = [(b, a) for a, b in ENTRY_FIRST]
EXIT_SECOND = [(b, a) for a, b in ENTRY_SECOND]


def swap(value, axis):
    return lax.ppermute(value, axis, [(0, 1), (1, 0)])


def pull(value, axis, distance):
    return lax.ppermute(value, axis, [((i + distance) % 4, i) for i in range(4)])


def place_in(block, home):
    widen = ((0, ROWS - HALF), (0, 0))
    first, second = jnp.pad(block[:HALF], widen), jnp.pad(block[HALF:], widen)
    moved = lax.ppermute(jnp.where(home, second, first), GROUP, ENTRY_FIRST)
    crossed = lax.ppermute(second, GROUP, ENTRY_SECOND)
    return jnp.concatenate(
        [jnp.where(home, first, moved), jnp.where(home, moved, crossed)], axis=1
    )


def place_out(values, home):
    own, other = values[:HALF, : D // 2], values[:HALF, D // 2 :].astype(BF)
    moved = lax.ppermute(jnp.where(home, other, own.astype(BF)), GROUP, EXIT_FIRST)
    crossed = lax.ppermute(other, GROUP, EXIT_SECOND)
    moved, crossed = moved.astype(F32), crossed.astype(F32)
    return jnp.concatenate([jnp.where(home, own, moved), jnp.where(home, moved, crossed)], axis=0)


def gather(piece):
    near = [piece] + [pull(piece, "y", d) for d in (1, 2, 3)]
    far = [swap(value, "c") for value in near]
    return jnp.concatenate(near + far, axis=0)


def scatter_sum(partial):
    half = NY * ROWS
    summed = partial[:half] + swap(partial[half:].astype(BF), "c").astype(F32)
    total = summed[:ROWS]
    for d in (1, 2, 3):
        piece = summed[d * ROWS : (d + 1) * ROWS].astype(BF)
        total = total + pull(piece, "y", -d).astype(F32)
    return total


def to_tokens(values):
    half = NY * ROWS
    both = jnp.concatenate([values[:half], swap(values[half:], "c")], axis=1)
    parts = [both[:ROWS]]
    for d in (1, 2, 3):
        e = (-d) % NY
        parts.append(pull(both[e * ROWS : (e + 1) * ROWS], "y", d))
    return jnp.concatenate(parts, axis=1)


def to_columns(values):
    width = values.shape[1] // NY
    parts = [values[:, :width]]
    for d in (1, 2, 3):
        e = (-d) % NY
        parts.append(pull(values[:, e * width : (e + 1) * width], "y", d))
    both = jnp.concatenate(parts, axis=0)
    return jnp.concatenate([both[:, : width // 2], swap(both[:, width // 2 :], "c")], axis=0)


def image_sum(own, other):
    return own + swap(other.astype(BF), "xh").astype(F32)


def replica_sum(values):
    rows = values.shape[0] // NZ
    z = lax.axis_index("z")

    def chunk(d):
        return lax.dynamic_slice_in_dim(values, ((z + d) % NZ) * rows, rows, 0)

    total = chunk(0)
    for d in (1, 2, 3):
        total = total + pull(chunk(d).astype(BF), "z", -d).astype(F32)
    total = total.astype(BF)
    total = (total.astype(F32) + swap(total, "xl").astype(F32)).astype(BF)
    out = jnp.zeros(values.shape, F32)
    for d in range(NZ):
        piece = total if d == 0 else pull(total, "z", d)
        out = lax.dynamic_update_slice_in_dim(out, piece.astype(F32), ((z + d) % NZ) * rows, 0)
    return out


def ring_sum(values, axis):
    opposite, after, before = (pull(values, axis, d) for d in (2, 1, 3))
    return (values + opposite) + (after + before)


def token_sum(values):
    return ring_sum(values + swap(values, "c"), "y")


def all_image_sum(own, other):
    values = own + swap(other, "xh")
    values = ring_sum(values, "z")
    return values + swap(values, "xl")


def dot(first, second, contract):
    return lax.dot_general(
        first, second, (((contract[0],), (contract[1],)), ((), ())), preferred_element_type=F32
    )


def norm(values, gain, shift):
    center = jnp.mean(values, axis=1, keepdims=True)
    moved = values - center
    inverse = lax.rsqrt(jnp.mean(moved * moved, axis=1, keepdims=True) + EPSILON)
    scaled = moved * inverse
    return (scaled * gain + shift).astype(BF), scaled, inverse


def norm_pull(grad, scaled, inverse, gain):
    weighted = grad * gain
    mean = jnp.mean(weighted, axis=1, keepdims=True)
    inner = jnp.mean(weighted * scaled, axis=1, keepdims=True)
    return inverse * (weighted - mean - scaled * inner)


def attend_scores(query, key, mask):
    scores = dot(query, key, (1, 1)) * (1.0 / math.sqrt(HD))
    return jnp.where(mask[None, :], scores, MASKED)


def attend(packed, mask):
    outs, logs = [], []
    for head in range(2):
        query, key, value = (
            packed[:, 128 * s + HD * head : 128 * s + HD * (head + 1)] for s in range(3)
        )
        scores = attend_scores(query, key, mask)
        highest = jnp.max(scores, axis=1, keepdims=True)
        weights = jnp.exp(scores - highest)
        total = jnp.sum(weights, axis=1, keepdims=True)
        outs.append(dot((weights / total).astype(BF), value, (1, 0)).astype(BF))
        logs.append(highest + jnp.log(total))
    return jnp.concatenate(outs, axis=1), logs


def attend_pull(packed, mask, logs, mixture_grad):
    grads = [[], [], []]
    factor = 1.0 / math.sqrt(HD)
    for head in range(2):
        query, key, value = (
            packed[:, 128 * s + HD * head : 128 * s + HD * (head + 1)] for s in range(3)
        )
        grad = mixture_grad[:, HD * head : HD * (head + 1)]
        chance = jnp.exp(attend_scores(query, key, mask) - logs[head])
        chance_grad = dot(grad, value, (1, 1))
        inner = jnp.sum(chance_grad * chance, axis=1, keepdims=True)
        score_grad = (chance * (chance_grad - inner)).astype(BF)
        grads[0].append(dot(score_grad, key, (1, 0)) * factor)
        grads[1].append(dot(score_grad, query, (0, 0)) * factor)
        grads[2].append(dot(chance.astype(BF), grad, (0, 0)))
    return jnp.concatenate(grads[0] + grads[1] + grads[2], axis=1).astype(BF)


def shards(
    inputs,
    w_qkv,
    qv_bias,
    w_out,
    w_fc1,
    fc1_bias,
    w_fc2,
    ln_gain,
    ln_bias,
    layer_scale,
    branch_bias,
    cotangent,
):
    r, y, c = (lax.axis_index(name) for name in GROUP)
    home = is_home(r, y)

    rows = jnp.concatenate([ln_gain[0], ln_bias[0], layer_scale[0], branch_bias[0]], axis=0)
    flat = jnp.concatenate([rows.reshape(-1), qv_bias.reshape(-1), fc1_bias.reshape(-1)])
    theirs = swap(flat.reshape(-1, 128), "xh").reshape(-1)
    count = rows.size
    rows = jnp.concatenate([rows, theirs[:count].reshape(rows.shape)], axis=1).astype(F32)
    gains, shifts, scales, biases = rows[0:2], rows[2:4], rows[4:6], rows[6:8]

    def in_order(mine, other):
        return jnp.where(r == 0, jnp.concatenate([mine, other]), jnp.concatenate([other, mine]))

    head_bias = in_order(flat[count : count + 128], theirs[count : count + 128])
    head_bias = head_bias.astype(F32).reshape(2, 2, HD)
    zeros = jnp.zeros((128,), F32)
    full_bias = jnp.concatenate([head_bias[:, 0].reshape(-1), zeros, head_bias[:, 1].reshape(-1)])
    unit_bias = in_order(flat[count + 128 :], theirs[count + 128 :]).astype(F32)

    x = place_in(inputs, home).astype(F32)
    qkv_weight = jnp.concatenate([w_qkv[0], swap(w_qkv[0], "xh")], axis=0)
    qkv_weight = qkv_weight.reshape(D, 2, 3, HD).transpose(0, 2, 1, 3).reshape(D, 6 * HD)
    upstream = place_in(cotangent, home).astype(F32)
    out_block = jnp.concatenate([w_out[0], swap(w_out[0], "xh")], axis=1)
    fc1_weight = jnp.concatenate([w_fc1[0], swap(w_fc1[0], "xh")], axis=0)
    fc2_weight = jnp.concatenate([w_fc2[0], swap(w_fc2[0], "xh")], axis=1)
    blocks = []
    for d in range(NY):
        near = out_block if d == 0 else pull(out_block, "y", d)
        blocks += [near, swap(near, "c")]
    out_weight = jnp.concatenate(blocks, axis=0)

    normed, scaled_first, inverse_first = norm(x, gains[0], shifts[0])
    normed_first = gather(normed)
    packed = (dot(normed_first, qkv_weight, (1, 0)) + full_bias).astype(BF)
    position = jnp.arange(SLOTS * ROWS)
    slot, local = position // ROWS, position % ROWS
    owner_y, owner_c = (y + slot % NY) % NY, c ^ (slot // NY)
    last = (owner_y == (2 * r + 3) % NY) & (owner_c == 1)
    mask = local < jnp.where(last, HALF - (8 * HALF - SEQ), HALF)
    mixture, logs = attend(packed, mask)
    mixture_tokens = to_tokens(mixture)
    branch_first = dot(mixture_tokens, out_weight, (1, 0)) + biases[0]
    x = x + scales[0] * branch_first

    normed, scaled_second, inverse_second = norm(x, gains[1], shifts[1])
    normed_second = gather(normed)
    hidden = dot(normed_second, fc1_weight, (1, 0)) + unit_bias
    spread = 0.5 * (1.0 + lax.erf(hidden * (1.0 / math.sqrt(2.0))))
    active = (hidden * spread).astype(BF)
    branch_second = scatter_sum(dot(active, fc2_weight, (1, 0))) + biases[1]
    output = place_out(x + scales[1] * branch_second, home)

    branch_grad = (upstream * scales[1]).astype(BF)
    branch_full = gather(branch_grad)
    active_grad = dot(branch_full, fc2_weight, (1, 1))
    slope = spread + hidden * jnp.exp(-0.5 * hidden * hidden) * (1.0 / math.sqrt(2.0 * math.pi))
    hidden_grad = (active_grad * slope).astype(BF)
    normed_grad = scatter_sum(dot(hidden_grad, fc1_weight, (1, 1)))
    fc2_grad = dot(active, branch_full, (0, 0))
    fc1_grad = dot(normed_second, hidden_grad, (0, 0))
    scale_second = jnp.sum(upstream * branch_second, axis=0)
    bias_second = jnp.sum(branch_grad.astype(F32), axis=0)
    gain_second = jnp.sum(normed_grad * scaled_second, axis=0)
    shift_second = jnp.sum(normed_grad, axis=0)
    unit_grad = jnp.sum(hidden_grad.astype(F32), axis=0)
    fc2_grad = replica_sum(image_sum(fc2_grad[:, : D // 2], fc2_grad[:, D // 2 :]))
    fc1_grad = replica_sum(image_sum(fc1_grad[: D // 2], fc1_grad[D // 2 :]))

    upstream = upstream + norm_pull(normed_grad, scaled_second, inverse_second, gains[1])
    scale_first = jnp.sum(upstream * branch_first, axis=0)
    branch_grad = (upstream * scales[0]).astype(BF)
    bias_first = jnp.sum(branch_grad.astype(F32), axis=0)
    mixture_grad = to_columns(dot(branch_grad, out_weight, (1, 1)).astype(BF))
    out_grad = dot(mixture, gather(branch_grad), (0, 0))
    out_grad = replica_sum(image_sum(out_grad[:, : D // 2], out_grad[:, D // 2 :]))
    packed_grad = attend_pull(packed, mask, logs, mixture_grad)
    normed_grad = scatter_sum(dot(packed_grad, qkv_weight, (1, 1)))
    head_grad = jnp.sum(packed_grad.astype(F32), axis=0).reshape(3, 2, HD)
    head_grad = jnp.stack([head_grad[0], head_grad[2]], axis=1).reshape(2, 128)
    qkv_grad = dot(normed_first, packed_grad, (0, 0))
    qkv_grad = qkv_grad.reshape(D, 3, 2, HD).transpose(0, 2, 1, 3).reshape(D, 6 * HD)
    qkv_grad = replica_sum(image_sum(qkv_grad[: D // 2], qkv_grad[D // 2 :]))
    gain_first = jnp.sum(normed_grad * scaled_first, axis=0)
    shift_first = jnp.sum(normed_grad, axis=0)
    input_grad = place_out(
        upstream + norm_pull(normed_grad, scaled_first, inverse_first, gains[0]), home
    )

    def pick(pair):
        return jnp.where(r == 0, pair[0], pair[1]), jnp.where(r == 0, pair[1], pair[0])

    early = jnp.stack(
        [gain_second, shift_second, scale_first, scale_second, bias_first, bias_second]
    )
    early = token_sum(early)
    unit_own, unit_other = pick(unit_grad.reshape(2, 2, 128))
    early = all_image_sum(
        jnp.concatenate([early[:, : D // 2].reshape(-1, 128), unit_own], axis=0),
        jnp.concatenate([early[:, D // 2 :].reshape(-1, 128), unit_other], axis=0),
    )
    unit_total = early[24:].reshape(1, 1, 1, -1)
    early = early[:24].reshape(6, D // 2)
    late = token_sum(jnp.stack([gain_first, shift_first]))
    head_own, head_other = pick(head_grad)
    late = all_image_sum(
        jnp.concatenate([late[:, : D // 2].reshape(-1, 128), head_own[None]], axis=0),
        jnp.concatenate([late[:, D // 2 :].reshape(-1, 128), head_other[None]], axis=0),
    )
    head_total = late[8:].reshape(1, 1, 1, 1, -1)
    late = late[:8].reshape(2, D // 2)
    return (
        output,
        input_grad,
        qkv_grad[None],
        head_total,
        out_grad[None],
        fc1_grad[None],
        unit_total,
        fc2_grad[None],
        jnp.stack([late[0], early[0]])[None],
        jnp.stack([late[1], early[1]])[None],
        early[2:4][None],
        early[4:6][None],
    )


def solution(mesh):
    fine = Mesh(mesh.devices.reshape(NZ, 2, 2, NY, 2), ("z", "xl") + GROUP)
    tokens = P(("z", "xl", "y", "c"), "xh")
    tall = P(None, "xh", ("y", "c"))
    wide = P(None, ("y", "c"), "xh")
    head = P(None, ("y", "c"), "xh", None, None)
    unit = P(None, ("y", "c"), "xh", None)
    vector = P(None, None, "xh")
    return jax.shard_map(
        shards,
        mesh=fine,
        in_specs=(
            tokens,
            tall,
            head,
            wide,
            tall,
            unit,
            wide,
            vector,
            vector,
            vector,
            vector,
            tokens,
        ),
        out_specs=(
            tokens,
            tokens,
            tall,
            head,
            wide,
            tall,
            unit,
            wide,
            vector,
            vector,
            vector,
            vector,
        ),
        check_vma=False,
    )
```

```python
import math

import jax
import jax.numpy as jnp
from jax import lax
from jax.sharding import Mesh, PartitionSpec as P

D = 1024
HD = 64
SEQ = 1025
EPSILON = 1e-06
MASKED = -1000000000.0

HALF = 129
ROWS = 136
SLOTS = 8
NY = 4
NZ = 4

F32 = jnp.float32
BF = jnp.bfloat16
GROUP = ("xh", "y", "c")


def is_home(r, y):
    return y // 2 == r


def group_index(r, y, c):
    return (r * NY + y % NY) * 2 + c


def entry_pairs():
    places = [(r, y, c) for r in range(2) for y in range(NY) for c in range(2)]
    first, second = [], []
    for r, y, c in places:
        me = group_index(r, y, c)
        if is_home(r, y):
            first.append((me, group_index(r, y + 2, c)))
        else:
            first.append((me, group_index(1 - r, y, c)))
            second.append((me, group_index(1 - r, y + 2, c)))
    return first, second


ENTRY_FIRST, ENTRY_SECOND = entry_pairs()
EXIT_FIRST = [(b, a) for a, b in ENTRY_FIRST]
EXIT_SECOND = [(b, a) for a, b in ENTRY_SECOND]


def swap(value, axis):
    return lax.ppermute(value, axis, [(0, 1), (1, 0)])


def pull(value, axis, distance):
    return lax.ppermute(value, axis, [((i + distance) % 4, i) for i in range(4)])


def after(value, *earlier):
    return lax.optimization_barrier((value,) + earlier)[0]


def place_in(block, spare, home):
    first = jnp.concatenate([block[:HALF], spare], axis=0)
    second = jnp.concatenate([block[HALF:], spare], axis=0)
    moved = lax.ppermute(jnp.where(home, second, first), GROUP, ENTRY_FIRST)
    crossed = lax.ppermute(second, GROUP, ENTRY_SECOND)
    own, other = jnp.where(home, first, moved), jnp.where(home, moved, crossed)
    tokens = jnp.concatenate([own, other], axis=1)
    real = jnp.arange(ROWS)[:, None] < HALF
    return jnp.where(real, tokens.astype(F32), 0.0), other[HALF:], (moved, crossed)


def place_out(values, home):
    own, other = values[:HALF, : D // 2], values[:HALF, D // 2 :].astype(BF)
    moved = lax.ppermute(jnp.where(home, other, own.astype(BF)), GROUP, EXIT_FIRST)
    crossed = lax.ppermute(other, GROUP, EXIT_SECOND)
    moved, crossed = moved.astype(F32), crossed.astype(F32)
    return jnp.concatenate([jnp.where(home, own, moved), jnp.where(home, moved, crossed)], axis=0)


def gather(piece):
    near = jnp.concatenate([piece] + [pull(piece, "y", d) for d in (1, 2, 3)], axis=0)
    return near, swap(near, "c")


def scatter_sum(halves, weight, contract):
    near, far = halves
    far = swap(dot(far, weight, contract).astype(BF), "c")
    summed = dot(near, weight, contract) + far.astype(F32)
    total = summed[:ROWS]
    for d in (1, 2, 3):
        piece = summed[d * ROWS : (d + 1) * ROWS].astype(BF)
        total = total + pull(piece, "y", -d).astype(F32)
    return total


def to_tokens(values):
    half = NY * ROWS
    both = jnp.concatenate([values[:half], swap(values[half:], "c")], axis=1)
    parts = [both[:ROWS]]
    for d in (1, 2, 3):
        e = (-d) % NY
        parts.append(pull(both[e * ROWS : (e + 1) * ROWS], "y", d))
    return jnp.concatenate(parts, axis=1)


def image_sum(own, other):
    return own + swap(other.astype(BF), "xh").astype(F32)


def replica_scatter(values):
    rows = values.shape[0] // NZ
    z = lax.axis_index("z")

    def chunk(d):
        return lax.dynamic_slice_in_dim(values, ((z + d) % NZ) * rows, rows, 0)

    total = chunk(0)
    for d in (1, 2, 3):
        total = total + pull(chunk(d).astype(BF), "z", -d).astype(F32)
    return total.astype(BF)


def replica_gather(total):
    z = lax.axis_index("z")
    total = (total.astype(F32) + swap(total, "xl").astype(F32)).astype(BF)
    pieces = [total] + [pull(total, "z", d) for d in (1, 2, 3)]

    def slot(k):
        d = (k - z) % NZ
        low = jnp.where(d == 0, pieces[0], pieces[1])
        return jnp.where(d < 2, low, jnp.where(d == 2, pieces[2], pieces[3])).astype(F32)

    return jnp.concatenate([slot(k) for k in range(NZ)], axis=0)


def column_sum(values):
    values = values + swap(values, "c")
    opposite, later, earlier = (pull(values, "y", d) for d in (2, 1, 3))
    return (values + opposite) + (later + earlier)


def dot(first, second, contract):
    return lax.dot_general(
        first, second, (((contract[0],), (contract[1],)), ((), ())), preferred_element_type=F32
    )


def norm(values, gain, shift):
    center = jnp.mean(values, axis=1, keepdims=True)
    moved = values - center
    inverse = lax.rsqrt(jnp.mean(moved * moved, axis=1, keepdims=True) + EPSILON)
    scaled = moved * inverse
    return (scaled * gain + shift).astype(BF), scaled, inverse


def norm_pull(grad, scaled, inverse, gain):
    weighted = grad * gain
    mean = jnp.mean(weighted, axis=1, keepdims=True)
    inner = jnp.mean(weighted * scaled, axis=1, keepdims=True)
    return inverse * (weighted - mean - scaled * inner)


def attend_scores(query, key, mask):
    scores = dot(query, key, (1, 1)) * (1.0 / math.sqrt(HD))
    return jnp.where(mask[None, :], scores, MASKED)


def attend(packed, mask):
    outs, logs = [], []
    for head in range(2):
        query, key, value = (
            packed[:, 128 * s + HD * head : 128 * s + HD * (head + 1)] for s in range(3)
        )
        scores = attend_scores(query, key, mask)
        highest = jnp.max(scores, axis=1, keepdims=True)
        weights = jnp.exp(scores - highest)
        total = jnp.sum(weights, axis=1, keepdims=True)
        outs.append(dot((weights / total).astype(BF), value, (1, 0)).astype(BF))
        logs.append(highest + jnp.log(total))
    return jnp.concatenate(outs, axis=1), logs


def attend_pull(packed, mask, logs, mixture_grad):
    grads = [[], [], []]
    factor = 1.0 / math.sqrt(HD)
    for head in range(2):
        query, key, value = (
            packed[:, 128 * s + HD * head : 128 * s + HD * (head + 1)] for s in range(3)
        )
        grad = mixture_grad[:, HD * head : HD * (head + 1)]
        chance = jnp.exp(attend_scores(query, key, mask) - logs[head])
        chance_grad = dot(grad, value, (1, 1))
        inner = jnp.sum(chance_grad * chance, axis=1, keepdims=True)
        score_grad = (chance * (chance_grad - inner)).astype(BF)
        grads[0].append(dot(score_grad, key, (1, 0)) * factor)
        grads[1].append(dot(score_grad, query, (0, 0)) * factor)
        grads[2].append(dot(chance.astype(BF), grad, (0, 0)))
    return jnp.concatenate(grads[0] + grads[1] + grads[2], axis=1).astype(BF)


def shards(
    inputs,
    w_qkv,
    qv_bias,
    w_out,
    w_fc1,
    fc1_bias,
    w_fc2,
    ln_gain,
    ln_bias,
    layer_scale,
    branch_bias,
    cotangent,
):
    r, y, c = (lax.axis_index(name) for name in GROUP)
    home = is_home(r, y)

    def in_order(mine, other):
        return jnp.where(r == 0, jnp.concatenate([mine, other]), jnp.concatenate([other, mine]))

    def pick(pair):
        return jnp.where(r == 0, pair[0], pair[1]), jnp.where(r == 0, pair[1], pair[0])

    own_rows = [ln_gain[0], ln_bias[0], layer_scale[0], branch_bias[0]]
    own_rows = jnp.concatenate(own_rows, axis=0)
    small = jnp.concatenate([qv_bias.reshape(-1), fc1_bias.reshape(-1)])
    spare = ROWS - HALF
    x, theirs, entered = place_in(inputs, own_rows[:spare], home)
    second_spare = jnp.pad(own_rows[spare:], ((0, spare - 1), (0, 0)))
    upstream, more, _ = place_in(after(cotangent, *entered), second_spare, home)
    rows = jnp.concatenate([own_rows, jnp.concatenate([theirs, more[:1]], axis=0)], axis=1)
    rows = rows.astype(F32)
    gains, shifts, scales, biases = rows[0:2], rows[2:4], rows[4:6], rows[6:8]
    qkv_other = jnp.concatenate([w_qkv[0], jnp.pad(small[None], ((0, 15), (0, 0)))], axis=0)
    qkv_other = swap(after(qkv_other, *entered), "xh")
    small_other, qkv_other = qkv_other[D // 2], qkv_other[: D // 2]
    qkv_weight = jnp.concatenate([w_qkv[0], qkv_other], axis=0)
    qkv_weight = qkv_weight.reshape(D, 2, 3, HD).transpose(0, 2, 1, 3).reshape(D, 6 * HD)
    out_start = after(w_out[0], entered[0])
    out_own = jnp.concatenate([out_start] + [pull(out_start, "y", d) for d in (1, 2, 3)], axis=0)
    out_other = swap(after(out_own, qkv_other), "xh")
    fc1_other = swap(after(w_fc1[0], out_other), "xh")
    fc2_other = swap(after(w_fc2[0], fc1_other), "xh")
    out_near = jnp.concatenate([out_own, out_other], axis=1)
    out_block = out_near[:128]
    out_weight = [out_near.reshape(NY, 128, D), swap(out_near, "c").reshape(NY, 128, D)]
    out_weight = jnp.stack(out_weight, axis=1)
    out_weight = out_weight.reshape(D, D)
    fc1_weight = jnp.concatenate([w_fc1[0], fc1_other], axis=0)
    fc2_weight = jnp.concatenate([w_fc2[0], fc2_other], axis=1)

    head_bias = in_order(small[:128], small_other[:128]).astype(F32).reshape(2, 2, HD)
    zeros = jnp.zeros((128,), F32)
    full_bias = jnp.concatenate([head_bias[:, 0].reshape(-1), zeros, head_bias[:, 1].reshape(-1)])
    unit_bias = in_order(small[128:], small_other[128:]).astype(F32)

    normed, scaled_first, inverse_first = norm(x, gains[0], shifts[0])
    normed_first = gather(normed)
    packed = [(dot(half, qkv_weight, (1, 0)) + full_bias).astype(BF) for half in normed_first]
    packed = jnp.concatenate(packed, axis=0)
    position = jnp.arange(SLOTS * ROWS)
    slot, local = position // ROWS, position % ROWS
    owner_y, owner_c = (y + slot % NY) % NY, c ^ (slot // NY)
    last = (owner_y == (2 * r + 3) % NY) & (owner_c == 1)
    mask = local < jnp.where(last, HALF - (8 * HALF - SEQ), HALF)
    mixture, logs = attend(packed, mask)
    last_grad = (upstream * scales[1]).astype(BF)
    last_full = gather(after(last_grad, normed_first[0]))
    mixture_tokens = to_tokens(after(mixture, *last_full))
    branch_first = dot(mixture_tokens, out_weight, (1, 0)) + biases[0]
    x = x + scales[0] * branch_first

    normed, scaled_second, inverse_second = norm(x, gains[1], shifts[1])
    normed_second = gather(normed)
    active, hidden_grad = [], []
    for half, grad in zip(normed_second, last_full):
        hidden = dot(half, fc1_weight, (1, 0)) + unit_bias
        spread = 0.5 * (1.0 + lax.erf(hidden * (1.0 / math.sqrt(2.0))))
        active.append((hidden * spread).astype(BF))
        slope = jnp.exp(-0.5 * hidden * hidden) * (1.0 / math.sqrt(2.0 * math.pi))
        slope = spread + hidden * slope
        hidden_grad.append((dot(grad, fc2_weight, (1, 1)) * slope).astype(BF))
    normed_grad = scatter_sum(hidden_grad, fc1_weight, (1, 1))
    fc2_grad = sum(dot(one, two, (0, 0)) for one, two in zip(active, last_full))
    fc1_grad = sum(dot(one, two, (0, 0)) for one, two in zip(normed_second, hidden_grad))
    unit_grad = sum(jnp.sum(half.astype(F32), axis=0) for half in hidden_grad)
    fc_own = jnp.concatenate([fc1_grad[: D // 2], fc2_grad[:, : D // 2]], axis=0)
    fc_other = jnp.concatenate([fc1_grad[D // 2 :], fc2_grad[:, D // 2 :]], axis=0)
    fc_sum = image_sum(fc_own, fc_other)
    scale_second = jnp.sum(fc2_weight.astype(F32) * fc2_grad, axis=0) / scales[1]
    scale_second = scale_second + biases[1] * jnp.sum(upstream, axis=0)

    upstream = upstream + norm_pull(normed_grad, scaled_second, inverse_second, gains[1])
    first_grad = (upstream * scales[0]).astype(BF)
    vectors = [
        jnp.sum(normed_grad * scaled_second, axis=0),
        jnp.sum(normed_grad, axis=0),
        jnp.sum(upstream * branch_first, axis=0),
        scale_second,
    ]
    carried = jnp.concatenate([first_grad[:HALF], jnp.stack(vectors).astype(BF)], axis=0)
    carried = gather(jnp.pad(carried, ((0, spare - 4), (0, 0))))
    fc_sum = replica_scatter(after(fc_sum, first_grad))
    real = jnp.arange(NY * ROWS)[:, None] % ROWS < HALF
    first_full = [jnp.where(real, half, jnp.zeros((), BF)) for half in carried]
    spares = [half.reshape(NY, ROWS, D)[:, HALF : HALF + 4].astype(F32) for half in carried]
    vectors = sum(jnp.sum(half, axis=0) for half in spares)
    bias_first = sum(jnp.sum(half.astype(F32), axis=0, keepdims=True) for half in first_full)
    bias_second = sum(jnp.sum(half.astype(F32), axis=0, keepdims=True) for half in last_full)
    vectors = jnp.concatenate([vectors, bias_first, bias_second], axis=0)

    mixture_grad = [dot(half, out_block, (1, 1)).astype(BF) for half in first_full]
    mixture_grad = after(jnp.concatenate(mixture_grad, axis=0), fc_sum)
    half_rows = NY * ROWS
    out_grad = dot(first_full[0], mixture[:half_rows], (0, 0))
    out_grad = out_grad + dot(first_full[1], mixture[half_rows:], (0, 0))
    active = [after(half, first_full[1]) for half in active]
    branch_second = scatter_sum(active, fc2_weight, (1, 0)) + biases[1]
    output = x + scales[1] * branch_second
    packed_grad = after(attend_pull(packed, mask, logs, mixture_grad), branch_second)
    packed_halves = packed_grad[:half_rows], packed_grad[half_rows:]
    normed_grad = scatter_sum(packed_halves, qkv_weight, (1, 1))
    output = place_out(after(output, packed_grad), home)
    fc_sum = replica_gather(after(fc_sum, packed_grad))

    qkv_grad = sum(dot(one, two, (0, 0)) for one, two in zip(normed_first, packed_halves))
    totals = jnp.sum(packed_grad.astype(F32), axis=0)
    wide_weight = qkv_weight.astype(F32)
    shift_part = jnp.sum(wide_weight * totals, axis=1)
    product = jnp.sum(wide_weight * qkv_grad, axis=1)
    gain_part = (product - shifts[0] * shift_part) / gains[0]
    late = jnp.concatenate([qkv_grad, out_grad], axis=1)
    head_grad = totals.reshape(3, 2, HD)
    head_grad = jnp.stack([head_grad[0], head_grad[2]], axis=1).reshape(2, 128)
    head_own, head_other = pick(head_grad)
    unit_own, unit_other = pick(unit_grad.reshape(2, 256))
    zeros = jnp.zeros((128,), F32)
    own = jnp.concatenate([unit_own, head_own, zeros])[None]
    other = jnp.concatenate([unit_other, head_other, zeros])[None]
    late_own = jnp.concatenate([late[: D // 2], vectors[:, : D // 2], own], axis=0)
    late_other = jnp.concatenate([late[D // 2 :], vectors[:, D // 2 :], other], axis=0)
    late = image_sum(late_own, late_other)
    final = column_sum(jnp.stack([gain_part, shift_part]))
    final = final[:, : D // 2] + swap(final[:, D // 2 :], "xh")
    late = jnp.concatenate([late, final, jnp.zeros((32 - 9, D // 2), F32)], axis=0)
    late = replica_gather(replica_scatter(late))
    input_grad = place_out(
        upstream + norm_pull(normed_grad, scaled_first, inverse_first, gains[0]), home
    )

    qkv_grad = late[: D // 2, :384].reshape(D // 2, 3, 2, HD).transpose(0, 2, 1, 3)
    out_grad = late[: D // 2, 384:].T
    vectors = late[D // 2 : D // 2 + 9]
    small = vectors[6]
    return (
        output,
        input_grad,
        qkv_grad.reshape(1, D // 2, 384),
        small[256:384].reshape(1, 1, 1, 1, -1),
        out_grad[None],
        fc_sum[None, : D // 2],
        small[:256].reshape(1, 1, 1, -1),
        fc_sum[None, D // 2 :],
        jnp.stack([vectors[7], vectors[0]])[None],
        jnp.stack([vectors[8], vectors[1]])[None],
        vectors[2:4][None],
        vectors[4:6][None],
    )


def solution(mesh):
    fine = Mesh(mesh.devices.reshape(NZ, 2, 2, NY, 2), ("z", "xl") + GROUP)
    tokens = P(("z", "xl", "y", "c"), "xh")
    tall = P(None, "xh", ("y", "c"))
    wide = P(None, ("y", "c"), "xh")
    head = P(None, ("y", "c"), "xh", None, None)
    unit = P(None, ("y", "c"), "xh", None)
    vector = P(None, None, "xh")
    return jax.shard_map(
        shards,
        mesh=fine,
        in_specs=(
            tokens,
            tall,
            head,
            wide,
            tall,
            unit,
            wide,
            vector,
            vector,
            vector,
            vector,
            tokens,
        ),
        out_specs=(
            tokens,
            tokens,
            tall,
            head,
            wide,
            tall,
            unit,
            wide,
            vector,
            vector,
            vector,
            vector,
        ),
        check_vma=False,
    )
```

```python
import math

import jax
import jax.numpy as jnp
from jax import lax
from jax.experimental import pallas as pl
from jax.experimental.pallas import tpu as pltpu
from jax.sharding import Mesh, PartitionSpec as P

D = 1024
HD = 64
SEQ = 1025
EPSILON = 1e-06
MASKED = -1000000000.0

HALF = 129
ROWS = 136
SLOTS = 8
NY = 4
NZ = 4

F32 = jnp.float32
BF = jnp.bfloat16
GROUP = ("xh", "y", "c")


def is_home(r, y):
    return y // 2 == r


def group_index(r, y, c):
    return (r * NY + y % NY) * 2 + c


def entry_pairs():
    places = [(r, y, c) for r in range(2) for y in range(NY) for c in range(2)]
    first, second = [], []
    for r, y, c in places:
        me = group_index(r, y, c)
        if is_home(r, y):
            first.append((me, group_index(r, y + 2, c)))
        else:
            first.append((me, group_index(1 - r, y, c)))
            second.append((me, group_index(1 - r, y + 2, c)))
    return first, second


ENTRY_FIRST, ENTRY_SECOND = entry_pairs()
EXIT_FIRST = [(b, a) for a, b in ENTRY_FIRST]
EXIT_SECOND = [(b, a) for a, b in ENTRY_SECOND]


def swap(value, axis):
    return lax.ppermute(value, axis, [(0, 1), (1, 0)])


def pull(value, axis, distance):
    return lax.ppermute(value, axis, [((i + distance) % 4, i) for i in range(4)])


def after(value, *earlier):
    return lax.optimization_barrier((value,) + earlier)[0]


def place_in(block, spare, home):
    first = jnp.concatenate([block[:HALF], spare], axis=0)
    second = jnp.concatenate([block[HALF:], spare], axis=0)
    moved = lax.ppermute(jnp.where(home, second, first), GROUP, ENTRY_FIRST)
    crossed = lax.ppermute(second, GROUP, ENTRY_SECOND)
    own, other = jnp.where(home, first, moved), jnp.where(home, moved, crossed)
    tokens = jnp.concatenate([own, other], axis=1)
    real = jnp.arange(ROWS)[:, None] < HALF
    return jnp.where(real, tokens.astype(F32), 0.0), other[HALF:], (moved, crossed)


def place_out(values, home):
    own, other = values[:HALF, : D // 2], values[:HALF, D // 2 :].astype(BF)
    moved = lax.ppermute(jnp.where(home, other, own.astype(BF)), GROUP, EXIT_FIRST)
    crossed = lax.ppermute(other, GROUP, EXIT_SECOND)
    moved, crossed = moved.astype(F32), crossed.astype(F32)
    return jnp.concatenate([jnp.where(home, own, moved), jnp.where(home, moved, crossed)], axis=0)


def gather(piece):
    near = jnp.concatenate([piece] + [pull(piece, "y", d) for d in (1, 2, 3)], axis=0)
    return near, swap(near, "c")


def scatter_begin(halves, weight, contract):
    near, far = halves
    far = swap(dot(far, weight, contract).astype(BF), "c")
    summed = dot(near, weight, contract) + far.astype(F32)
    return summed[:ROWS], [summed[d * ROWS : (d + 1) * ROWS].astype(BF) for d in (1, 2, 3)]


def scatter_end(total, pieces):
    for d, piece in zip((1, 2, 3), pieces):
        total = total + pull(piece, "y", -d).astype(F32)
    return total


def to_tokens(values):
    half = NY * ROWS
    both = jnp.concatenate([values[:half], swap(values[half:], "c")], axis=1)
    parts = [both[:ROWS]]
    for d in (1, 2, 3):
        e = (-d) % NY
        parts.append(pull(both[e * ROWS : (e + 1) * ROWS], "y", d))
    return jnp.concatenate(parts, axis=1)


def image_sum(own, other):
    return own + swap(other.astype(BF), "xh").astype(F32)


def replica_scatter(values):
    rows = values.shape[0] // NZ
    z = lax.axis_index("z")

    def chunk(d):
        return lax.dynamic_slice_in_dim(values, ((z + d) % NZ) * rows, rows, 0)

    total = chunk(0)
    for d in (1, 2, 3):
        total = total + pull(chunk(d).astype(BF), "z", -d).astype(F32)
    return total.astype(BF)


def replica_gather(total):
    z = lax.axis_index("z")
    total = (total.astype(F32) + swap(total, "xl").astype(F32)).astype(BF)
    pieces = [total] + [pull(total, "z", d) for d in (1, 2, 3)]

    def slot(k):
        d = (k - z) % NZ
        low = jnp.where(d == 0, pieces[0], pieces[1])
        return jnp.where(d < 2, low, jnp.where(d == 2, pieces[2], pieces[3])).astype(F32)

    return jnp.concatenate([slot(k) for k in range(NZ)], axis=0)


def column_sum(values):
    values = values + swap(values, "c")
    opposite, later, earlier = (pull(values, "y", d) for d in (2, 1, 3))
    return (values + opposite) + (later + earlier)


def dot(first, second, contract):
    return lax.dot_general(
        first, second, (((contract[0],), (contract[1],)), ((), ())), preferred_element_type=F32
    )


def norm(values, gain, shift):
    center = jnp.mean(values, axis=1, keepdims=True)
    moved = values - center
    inverse = lax.rsqrt(jnp.mean(moved * moved, axis=1, keepdims=True) + EPSILON)
    scaled = moved * inverse
    return (scaled * gain + shift).astype(BF), scaled, inverse


def norm_pull(grad, scaled, inverse, gain):
    weighted = grad * gain
    mean = jnp.mean(weighted, axis=1, keepdims=True)
    inner = jnp.mean(weighted * scaled, axis=1, keepdims=True)
    return inverse * (weighted - mean - scaled * inner)


BLOCK = 272


def chances(query, key, mask):
    scores = dot(query * (1.0 / math.sqrt(HD)), key, (1, 1))
    scores = jnp.where(mask > 0, scores, MASKED)
    weights = jnp.exp(scores - jnp.max(scores, axis=1, keepdims=True))
    return weights * (1.0 / jnp.sum(weights, axis=1, keepdims=True))


def attend_kernel(mask_ref, packed_ref, out_ref):
    mask = mask_ref[...]
    for head in range(2):
        part = [slice(128 * s + HD * head, 128 * s + HD * (head + 1)) for s in range(3)]
        key, value = packed_ref[:, part[1]], packed_ref[:, part[2]]
        for block in range(SLOTS * ROWS // BLOCK):
            rows = slice(block * BLOCK, (block + 1) * BLOCK)
            chance = chances(packed_ref[rows, part[0]], key, mask).astype(BF)
            out_ref[rows, part[0]] = dot(chance, value, (1, 0)).astype(BF)


def attend_pull_kernel(mask_ref, packed_ref, grad_ref, out_ref):
    mask = mask_ref[...]
    factor = 1.0 / math.sqrt(HD)
    for head in range(2):
        part = [slice(128 * s + HD * head, 128 * s + HD * (head + 1)) for s in range(3)]
        key, value = packed_ref[:, part[1]], packed_ref[:, part[2]]
        key_grad = jnp.zeros((SLOTS * ROWS, HD), F32)
        value_grad = jnp.zeros((SLOTS * ROWS, HD), F32)
        for block in range(SLOTS * ROWS // BLOCK):
            rows = slice(block * BLOCK, (block + 1) * BLOCK)
            query, grad = packed_ref[rows, part[0]], grad_ref[rows, part[0]]
            chance = chances(query, key, mask)
            chance_grad = dot(grad, value, (1, 1))
            inner = jnp.sum(chance_grad * chance, axis=1, keepdims=True)
            score_grad = (chance * (chance_grad - inner)).astype(BF)
            out_ref[rows, part[0]] = (dot(score_grad, key, (1, 0)) * factor).astype(BF)
            key_grad = key_grad + dot(score_grad, query, (0, 0))
            value_grad = value_grad + dot(chance.astype(BF), grad, (0, 0))
        out_ref[:, part[1]] = (key_grad * factor).astype(BF)
        out_ref[:, part[2]] = value_grad.astype(BF)


def local_kernel(kernel, width, micros, *operands):
    return pl.pallas_call(
        kernel,
        out_shape=jax.ShapeDtypeStruct((SLOTS * ROWS, width), BF),
        in_specs=[pl.BlockSpec(memory_space=pltpu.VMEM)] * len(operands),
        out_specs=pl.BlockSpec(memory_space=pltpu.VMEM),
        compiler_params=pltpu.CompilerParams(vmem_limit_bytes=32 * 1024 * 1024),
        cost_estimate=pl.CostEstimate(
            flops=micros * 1000000000, bytes_accessed=micros * 3000000, transcendentals=0
        ),
    )(*operands)


def attend(packed, mask):
    return local_kernel(attend_kernel, 2 * HD, 8, mask, packed)


def attend_pull(packed, mask, mixture_grad):
    return local_kernel(attend_pull_kernel, 6 * HD, 12, mask, packed, mixture_grad)


def shards(
    inputs,
    w_qkv,
    qv_bias,
    w_out,
    w_fc1,
    fc1_bias,
    w_fc2,
    ln_gain,
    ln_bias,
    layer_scale,
    branch_bias,
    cotangent,
):
    r, y, c = (lax.axis_index(name) for name in GROUP)
    home = is_home(r, y)

    def in_order(mine, other):
        return jnp.where(r == 0, jnp.concatenate([mine, other]), jnp.concatenate([other, mine]))

    def pick(pair):
        return jnp.where(r == 0, pair[0], pair[1]), jnp.where(r == 0, pair[1], pair[0])

    own_rows = [ln_gain[0], ln_bias[0], layer_scale[0], branch_bias[0]]
    own_rows = jnp.concatenate(own_rows, axis=0)
    small = jnp.concatenate([qv_bias.reshape(-1), fc1_bias.reshape(-1)])
    spare = ROWS - HALF
    x, theirs, entered = place_in(inputs, own_rows[:spare], home)
    second_spare = jnp.pad(own_rows[spare:], ((0, spare - 1), (0, 0)))
    upstream, more, _ = place_in(after(cotangent, *entered), second_spare, home)
    rows = jnp.concatenate([own_rows, jnp.concatenate([theirs, more[:1]], axis=0)], axis=1)
    rows = rows.astype(F32)
    gains, shifts, scales, biases = rows[0:2], rows[2:4], rows[4:6], rows[6:8]
    qkv_other = jnp.concatenate([w_qkv[0], jnp.pad(small[None], ((0, 15), (0, 0)))], axis=0)
    qkv_other = swap(after(qkv_other, *entered), "xh")
    small_other, qkv_other = qkv_other[D // 2], qkv_other[: D // 2]
    qkv_weight = jnp.concatenate([w_qkv[0], qkv_other], axis=0)
    qkv_weight = qkv_weight.reshape(D, 2, 3, HD).transpose(0, 2, 1, 3).reshape(D, 6 * HD)
    out_start = after(w_out[0], *entered)
    out_own = jnp.concatenate([out_start] + [pull(out_start, "y", d) for d in (1, 2, 3)], axis=0)
    out_other = swap(after(out_own, qkv_other), "xh")
    fc1_other = swap(after(w_fc1[0], out_other), "xh")
    fc2_other = swap(after(w_fc2[0], fc1_other), "xh")
    out_near = jnp.concatenate([out_own, out_other], axis=1)
    out_block = out_near[:128]
    out_weight = [out_near.reshape(NY, 128, D), swap(out_near, "c").reshape(NY, 128, D)]
    out_weight = jnp.stack(out_weight, axis=1)
    out_weight = out_weight.reshape(D, D)
    fc1_weight = jnp.concatenate([w_fc1[0], fc1_other], axis=0)
    fc2_weight = jnp.concatenate([w_fc2[0], fc2_other], axis=1)

    head_bias = in_order(small[:128], small_other[:128]).astype(F32).reshape(2, 2, HD)
    zeros = jnp.zeros((128,), F32)
    full_bias = jnp.concatenate([head_bias[:, 0].reshape(-1), zeros, head_bias[:, 1].reshape(-1)])
    unit_bias = in_order(small[128:], small_other[128:]).astype(F32)

    normed, scaled_first, inverse_first = norm(x, gains[0], shifts[0])
    normed_first = gather(normed)
    packed = [(dot(half, qkv_weight, (1, 0)) + full_bias).astype(BF) for half in normed_first]
    packed = jnp.concatenate(packed, axis=0)
    position = jnp.arange(SLOTS * ROWS)
    slot, local = position // ROWS, position % ROWS
    owner_y, owner_c = (y + slot % NY) % NY, c ^ (slot // NY)
    last = (owner_y == (2 * r + 3) % NY) & (owner_c == 1)
    mask = local < jnp.where(last, HALF - (8 * HALF - SEQ), HALF)
    mask = mask.astype(F32)[None]
    mixture = attend(packed, mask)
    last_grad = (upstream * scales[1]).astype(BF)
    last_full = gather(after(last_grad, normed_first[0]))
    mixture_tokens = to_tokens(after(mixture, *last_full))
    branch_first = dot(mixture_tokens, out_weight, (1, 0)) + biases[0]
    x = x + scales[0] * branch_first

    normed, scaled_second, inverse_second = norm(x, gains[1], shifts[1])
    normed_second = gather(normed)
    active, hidden_grad = [], []
    for half, grad in zip(normed_second, last_full):
        hidden = dot(half, fc1_weight, (1, 0)) + unit_bias
        spread = 0.5 * (1.0 + lax.erf(hidden * (1.0 / math.sqrt(2.0))))
        active.append((hidden * spread).astype(BF))
        slope = jnp.exp(-0.5 * hidden * hidden) * (1.0 / math.sqrt(2.0 * math.pi))
        slope = spread + hidden * slope
        hidden_grad.append((dot(grad, fc2_weight, (1, 1)) * slope).astype(BF))
    begun, sent = scatter_begin(hidden_grad, fc1_weight, (1, 1))
    normed_grad = scatter_end(begun, sent)
    fc2_grad = sum(dot(one, two, (0, 0)) for one, two in zip(active, last_full))
    fc1_grad = sum(dot(one, two, (0, 0)) for one, two in zip(normed_second, hidden_grad))
    unit_grad = sum(jnp.sum(half.astype(F32), axis=0) for half in hidden_grad)
    fc2_sum = replica_scatter(image_sum(fc2_grad[:, : D // 2], fc2_grad[:, D // 2 :]))
    fc1_sum = image_sum(fc1_grad[: D // 2], fc1_grad[D // 2 :])
    scale_second = jnp.sum(fc2_weight.astype(F32) * fc2_grad, axis=0) / scales[1]
    scale_second = scale_second + biases[1] * jnp.sum(upstream, axis=0)

    upstream = upstream + norm_pull(normed_grad, scaled_second, inverse_second, gains[1])
    first_grad = after((upstream * scales[0]).astype(BF), fc2_sum)
    vectors = [
        jnp.sum(normed_grad * scaled_second, axis=0),
        jnp.sum(normed_grad, axis=0),
        jnp.sum(upstream * branch_first, axis=0),
        scale_second,
    ]
    carried = jnp.concatenate([first_grad[:HALF], jnp.stack(vectors).astype(BF)], axis=0)
    carried = gather(jnp.pad(carried, ((0, spare - 4), (0, 0))))
    fc1_sum = replica_scatter(after(fc1_sum, first_grad))
    fc2_sum = replica_gather(after(fc2_sum, first_grad))
    real = jnp.arange(NY * ROWS)[:, None] % ROWS < HALF
    first_full = [jnp.where(real, half, jnp.zeros((), BF)) for half in carried]
    spares = [half.reshape(NY, ROWS, D)[:, HALF : HALF + 4].astype(F32) for half in carried]
    vectors = sum(jnp.sum(half, axis=0) for half in spares)
    bias_first = sum(jnp.sum(half.astype(F32), axis=0, keepdims=True) for half in first_full)
    bias_second = sum(jnp.sum(half.astype(F32), axis=0, keepdims=True) for half in last_full)
    vectors = jnp.concatenate([vectors, bias_first, bias_second], axis=0)

    mixture_grad = [dot(half, out_block, (1, 1)).astype(BF) for half in first_full]
    mixture_grad = jnp.concatenate(mixture_grad, axis=0)
    half_rows = NY * ROWS
    out_grad = dot(first_full[0], mixture[:half_rows], (0, 0))
    out_grad = out_grad + dot(first_full[1], mixture[half_rows:], (0, 0))
    packed_grad = after(attend_pull(packed, mask, mixture_grad), fc1_sum, fc2_sum)
    packed_halves = packed_grad[:half_rows], packed_grad[half_rows:]
    begun, sent = scatter_begin(packed_halves, qkv_weight, (1, 1))
    normed_grad = scatter_end(begun, sent)
    fc1_sum = replica_gather(after(fc1_sum, *sent))
    active = [after(half, normed_grad) for half in active]
    branch_second = scatter_end(*scatter_begin(active, fc2_weight, (1, 0))) + biases[1]
    output = place_out(x + scales[1] * branch_second, home)

    qkv_grad = sum(dot(one, two, (0, 0)) for one, two in zip(normed_first, packed_halves))
    totals = jnp.sum(packed_grad.astype(F32), axis=0)
    wide_weight = qkv_weight.astype(F32)
    shift_part = jnp.sum(wide_weight * totals, axis=1)
    product = jnp.sum(wide_weight * qkv_grad, axis=1)
    gain_part = (product - shifts[0] * shift_part) / gains[0]
    late = jnp.concatenate([qkv_grad, out_grad], axis=1)
    head_grad = totals.reshape(3, 2, HD)
    head_grad = jnp.stack([head_grad[0], head_grad[2]], axis=1).reshape(2, 128)
    head_own, head_other = pick(head_grad)
    unit_own, unit_other = pick(unit_grad.reshape(2, 256))
    zeros = jnp.zeros((128,), F32)
    own = jnp.concatenate([unit_own, head_own, zeros])[None]
    other = jnp.concatenate([unit_other, head_other, zeros])[None]
    late_own = jnp.concatenate([late[: D // 2], vectors[:, : D // 2], own], axis=0)
    late_other = jnp.concatenate([late[D // 2 :], vectors[:, D // 2 :], other], axis=0)
    late = image_sum(late_own, late_other)
    final = column_sum(jnp.stack([gain_part, shift_part]))
    final = final[:, : D // 2] + swap(final[:, D // 2 :], "xh")
    late = jnp.concatenate([late, final, jnp.zeros((32 - 9, D // 2), F32)], axis=0)
    late = replica_scatter(after(late, fc1_sum, *sent))
    late = replica_gather(after(late, normed_grad))
    input_grad = place_out(
        upstream + norm_pull(normed_grad, scaled_first, inverse_first, gains[0]), home
    )

    qkv_grad = late[: D // 2, :384].reshape(D // 2, 3, 2, HD).transpose(0, 2, 1, 3)
    out_grad = late[: D // 2, 384:].T
    vectors = late[D // 2 : D // 2 + 9]
    small = vectors[6]
    return (
        output,
        input_grad,
        qkv_grad.reshape(1, D // 2, 384),
        small[256:384].reshape(1, 1, 1, 1, -1),
        out_grad[None],
        fc1_sum[None],
        small[:256].reshape(1, 1, 1, -1),
        fc2_sum[None],
        jnp.stack([vectors[7], vectors[0]])[None],
        jnp.stack([vectors[8], vectors[1]])[None],
        vectors[2:4][None],
        vectors[4:6][None],
    )


def solution(mesh):
    fine = Mesh(mesh.devices.reshape(NZ, 2, 2, NY, 2), ("z", "xl") + GROUP)
    tokens = P(("z", "xl", "y", "c"), "xh")
    tall = P(None, "xh", ("y", "c"))
    wide = P(None, ("y", "c"), "xh")
    head = P(None, ("y", "c"), "xh", None, None)
    unit = P(None, ("y", "c"), "xh", None)
    vector = P(None, None, "xh")
    return jax.shard_map(
        shards,
        mesh=fine,
        in_specs=(
            tokens,
            tall,
            head,
            wide,
            tall,
            unit,
            wide,
            vector,
            vector,
            vector,
            vector,
            tokens,
        ),
        out_specs=(
            tokens,
            tokens,
            tall,
            head,
            wide,
            tall,
            unit,
            wide,
            vector,
            vector,
            vector,
            vector,
        ),
        check_vma=False,
    )
```

```python
import math

import jax
import jax.numpy as jnp
from jax import lax
from jax.experimental import pallas as pl
from jax.experimental.pallas import tpu as pltpu
from jax.sharding import Mesh, PartitionSpec as P

D = 1024
HD = 64
SEQ = 1025
EPSILON = 1e-06
MASKED = -1000000000.0

HALF = 129
ROWS = 136
SLOTS = 8
NY = 4
NZ = 4

F32 = jnp.float32
BF = jnp.bfloat16
GROUP = ("xh", "y", "c")


def is_home(r, y):
    return y // 2 == r


def group_index(r, y, c):
    return (r * NY + y % NY) * 2 + c


def entry_pairs():
    places = [(r, y, c) for r in range(2) for y in range(NY) for c in range(2)]
    first, second = [], []
    for r, y, c in places:
        me = group_index(r, y, c)
        if is_home(r, y):
            first.append((me, group_index(r, y + 2, c)))
        else:
            first.append((me, group_index(1 - r, y, c)))
            second.append((me, group_index(1 - r, y + 2, c)))
    return first, second


ENTRY_FIRST, ENTRY_SECOND = entry_pairs()
EXIT_FIRST = [(b, a) for a, b in ENTRY_FIRST]
EXIT_SECOND = [(b, a) for a, b in ENTRY_SECOND]


def swap(value, axis):
    return lax.ppermute(value, axis, [(0, 1), (1, 0)])


def pull(value, axis, distance):
    return lax.ppermute(value, axis, [((i + distance) % 4, i) for i in range(4)])


def after(value, *earlier):
    return lax.optimization_barrier((value,) + earlier)[0]


def place_in(block, spare, home):
    first = jnp.concatenate([block[:HALF], spare], axis=0)
    second = jnp.concatenate([block[HALF:], spare], axis=0)
    moved = lax.ppermute(jnp.where(home, second, first), GROUP, ENTRY_FIRST)
    crossed = lax.ppermute(second, GROUP, ENTRY_SECOND)
    own, other = jnp.where(home, first, moved), jnp.where(home, moved, crossed)
    tokens = jnp.concatenate([own, other], axis=1)
    real = jnp.arange(ROWS)[:, None] < HALF
    return jnp.where(real, tokens.astype(F32), 0.0), other[HALF:], (moved, crossed)


def place_out(values, home):
    own, other = values[:HALF, : D // 2], values[:HALF, D // 2 :].astype(BF)
    moved = lax.ppermute(jnp.where(home, other, own.astype(BF)), GROUP, EXIT_FIRST)
    crossed = lax.ppermute(other, GROUP, EXIT_SECOND)
    moved, crossed = moved.astype(F32), crossed.astype(F32)
    return jnp.concatenate([jnp.where(home, own, moved), jnp.where(home, moved, crossed)], axis=0)


def gather(piece):
    near = jnp.concatenate([piece] + [pull(piece, "y", d) for d in (1, 2, 3)], axis=0)
    return near, swap(near, "c")


def scatter_begin(halves, weight, contract):
    near, far = halves
    far = swap(dot(far, weight, contract).astype(BF), "c")
    summed = dot(near, weight, contract) + far.astype(F32)
    return summed[:ROWS], [summed[d * ROWS : (d + 1) * ROWS].astype(BF) for d in (1, 2, 3)]


def scatter_end(total, pieces):
    for d, piece in zip((1, 2, 3), pieces):
        total = total + pull(piece, "y", -d).astype(F32)
    return total


def to_tokens(values):
    half = NY * ROWS
    both = jnp.concatenate([values[:half], swap(values[half:], "c")], axis=1)
    parts = [both[:ROWS]]
    for d in (1, 2, 3):
        e = (-d) % NY
        parts.append(pull(both[e * ROWS : (e + 1) * ROWS], "y", d))
    return jnp.concatenate(parts, axis=1)


def image_sum(own, other):
    return own + swap(other.astype(BF), "xh").astype(F32)


def replica_scatter(values):
    rows = values.shape[0] // NZ
    z = lax.axis_index("z")

    def chunk(d):
        return lax.dynamic_slice_in_dim(values, ((z + d) % NZ) * rows, rows, 0)

    total = chunk(0)
    for d in (1, 2, 3):
        total = total + pull(chunk(d).astype(BF), "z", -d).astype(F32)
    return total.astype(BF)


def replica_gather(total):
    z = lax.axis_index("z")
    total = (total.astype(F32) + swap(total, "xl").astype(F32)).astype(BF)
    pieces = [total] + [pull(total, "z", d) for d in (1, 2, 3)]

    def slot(k):
        d = (k - z) % NZ
        low = jnp.where(d == 0, pieces[0], pieces[1])
        return jnp.where(d < 2, low, jnp.where(d == 2, pieces[2], pieces[3])).astype(F32)

    return jnp.concatenate([slot(k) for k in range(NZ)], axis=0)


def column_sum(values):
    values = values + swap(values, "c")
    opposite, later, earlier = (pull(values, "y", d) for d in (2, 1, 3))
    return (values + opposite) + (later + earlier)


def dot(first, second, contract):
    return lax.dot_general(
        first, second, (((contract[0],), (contract[1],)), ((), ())), preferred_element_type=F32
    )


def norm(values, gain, shift):
    center = jnp.mean(values, axis=1, keepdims=True)
    moved = values - center
    inverse = lax.rsqrt(jnp.mean(moved * moved, axis=1, keepdims=True) + EPSILON)
    scaled = moved * inverse
    return (scaled * gain + shift).astype(BF), scaled, inverse


def norm_pull(grad, scaled, inverse, gain):
    weighted = grad * gain
    mean = jnp.mean(weighted, axis=1, keepdims=True)
    inner = jnp.mean(weighted * scaled, axis=1, keepdims=True)
    return inverse * (weighted - mean - scaled * inner)


BLOCK = 272


def chances(query, key, mask):
    scores = dot(query * (1.0 / math.sqrt(HD)), key, (1, 1))
    scores = jnp.where(mask > 0, scores, MASKED)
    weights = jnp.exp(scores - jnp.max(scores, axis=1, keepdims=True))
    return weights * (1.0 / jnp.sum(weights, axis=1, keepdims=True))


def attend_kernel(mask_ref, packed_ref, out_ref):
    mask = mask_ref[...]
    for head in range(2):
        part = [slice(128 * s + HD * head, 128 * s + HD * (head + 1)) for s in range(3)]
        key, value = packed_ref[:, part[1]], packed_ref[:, part[2]]
        for block in range(SLOTS * ROWS // BLOCK):
            rows = slice(block * BLOCK, (block + 1) * BLOCK)
            chance = chances(packed_ref[rows, part[0]], key, mask).astype(BF)
            out_ref[rows, part[0]] = dot(chance, value, (1, 0)).astype(BF)


def attend_pull_kernel(mask_ref, packed_ref, grad_ref, out_ref):
    mask = mask_ref[...]
    factor = 1.0 / math.sqrt(HD)
    for head in range(2):
        part = [slice(128 * s + HD * head, 128 * s + HD * (head + 1)) for s in range(3)]
        key, value = packed_ref[:, part[1]], packed_ref[:, part[2]]
        key_grad = jnp.zeros((SLOTS * ROWS, HD), F32)
        value_grad = jnp.zeros((SLOTS * ROWS, HD), F32)
        for block in range(SLOTS * ROWS // BLOCK):
            rows = slice(block * BLOCK, (block + 1) * BLOCK)
            query, grad = packed_ref[rows, part[0]], grad_ref[rows, part[0]]
            chance = chances(query, key, mask)
            chance_grad = dot(grad, value, (1, 1))
            inner = jnp.sum(chance_grad * chance, axis=1, keepdims=True)
            score_grad = (chance * (chance_grad - inner)).astype(BF)
            out_ref[rows, part[0]] = (dot(score_grad, key, (1, 0)) * factor).astype(BF)
            key_grad = key_grad + dot(score_grad, query, (0, 0))
            value_grad = value_grad + dot(chance.astype(BF), grad, (0, 0))
        out_ref[:, part[1]] = (key_grad * factor).astype(BF)
        out_ref[:, part[2]] = value_grad.astype(BF)


def local_kernel(kernel, width, micros, *operands):
    return pl.pallas_call(
        kernel,
        out_shape=jax.ShapeDtypeStruct((SLOTS * ROWS, width), BF),
        in_specs=[pl.BlockSpec(memory_space=pltpu.VMEM)] * len(operands),
        out_specs=pl.BlockSpec(memory_space=pltpu.VMEM),
        compiler_params=pltpu.CompilerParams(vmem_limit_bytes=32 * 1024 * 1024),
        cost_estimate=pl.CostEstimate(
            flops=micros * 1000000000, bytes_accessed=micros * 3000000, transcendentals=0
        ),
    )(*operands)


def attend(packed, mask):
    return local_kernel(attend_kernel, 2 * HD, 8, mask, packed)


def attend_pull(packed, mask, mixture_grad):
    return local_kernel(attend_pull_kernel, 6 * HD, 12, mask, packed, mixture_grad)


def shards(
    inputs,
    w_qkv,
    qv_bias,
    w_out,
    w_fc1,
    fc1_bias,
    w_fc2,
    ln_gain,
    ln_bias,
    layer_scale,
    branch_bias,
    cotangent,
):
    r, y, c = (lax.axis_index(name) for name in GROUP)
    home = is_home(r, y)

    def in_order(mine, other):
        return jnp.where(r == 0, jnp.concatenate([mine, other]), jnp.concatenate([other, mine]))

    def pick(pair):
        return jnp.where(r == 0, pair[0], pair[1]), jnp.where(r == 0, pair[1], pair[0])

    own_rows = [ln_gain[0], ln_bias[0], layer_scale[0], branch_bias[0]]
    own_rows = jnp.concatenate(own_rows, axis=0)
    small = jnp.concatenate([qv_bias.reshape(-1), fc1_bias.reshape(-1)])
    spare = ROWS - HALF
    x, theirs, entered = place_in(inputs, own_rows[:spare], home)
    second_spare = jnp.pad(own_rows[spare:], ((0, spare - 1), (0, 0)))
    upstream, more, _ = place_in(after(cotangent, *entered), second_spare, home)
    rows = jnp.concatenate([own_rows[:spare], theirs], axis=1).astype(F32)
    gains, shifts, scales, first_bias = rows[0:2], rows[2:4], rows[4:6], rows[6:7]
    second_bias = jnp.concatenate([own_rows[spare:], more[:1]], axis=1).astype(F32)
    qkv_other = jnp.concatenate([w_qkv[0], jnp.pad(small[None], ((0, 15), (0, 0)))], axis=0)
    qkv_other = swap(after(qkv_other, *entered), "xh")
    small_other, qkv_other = qkv_other[D // 2], qkv_other[: D // 2]
    qkv_weight = jnp.concatenate([w_qkv[0], qkv_other], axis=0)
    qkv_weight = qkv_weight.reshape(D, 2, 3, HD).transpose(0, 2, 1, 3).reshape(D, 6 * HD)
    normed, scaled_first, inverse_first = norm(x, gains[0], shifts[0])
    normed_first = gather(normed)
    out_start = after(w_out[0], normed_first[0])
    out_own = jnp.concatenate([out_start] + [pull(out_start, "y", d) for d in (1, 2, 3)], axis=0)
    out_other = swap(out_own, "xh")
    fc_other = jnp.concatenate([w_fc1[0], w_fc2[0]], axis=0)
    fc_other = swap(after(fc_other, qkv_other), "xh")
    fc1_other, fc2_other = fc_other[: D // 2], fc_other[D // 2 :]
    out_near = jnp.concatenate([out_own, out_other], axis=1)
    out_block = out_near[:128]
    out_weight = [out_near.reshape(NY, 128, D), swap(out_near, "c").reshape(NY, 128, D)]
    out_weight = jnp.stack(out_weight, axis=1)
    out_weight = out_weight.reshape(D, D)
    fc1_weight = jnp.concatenate([w_fc1[0], fc1_other], axis=0)
    fc2_weight = jnp.concatenate([w_fc2[0], fc2_other], axis=1)

    head_bias = in_order(small[:128], small_other[:128]).astype(F32).reshape(2, 2, HD)
    zeros = jnp.zeros((128,), F32)
    full_bias = jnp.concatenate([head_bias[:, 0].reshape(-1), zeros, head_bias[:, 1].reshape(-1)])
    unit_bias = in_order(small[128:], small_other[128:]).astype(F32)

    packed = [(dot(half, qkv_weight, (1, 0)) + full_bias).astype(BF) for half in normed_first]
    packed = jnp.concatenate(packed, axis=0)
    position = jnp.arange(SLOTS * ROWS)
    slot, local = position // ROWS, position % ROWS
    owner_y, owner_c = (y + slot % NY) % NY, c ^ (slot // NY)
    last = (owner_y == (2 * r + 3) % NY) & (owner_c == 1)
    mask = local < jnp.where(last, HALF - (8 * HALF - SEQ), HALF)
    mask = mask.astype(F32)[None]
    mixture = attend(packed, mask)
    last_grad = (upstream * scales[1]).astype(BF)
    last_full = gather(after(last_grad, normed_first[0]))
    mixture_tokens = to_tokens(mixture)
    branch_first = dot(mixture_tokens, out_weight, (1, 0)) + first_bias
    x = x + scales[0] * branch_first

    normed, scaled_second, inverse_second = norm(x, gains[1], shifts[1])
    normed_second = gather(after(normed, fc_other, *last_full))
    active, hidden_grad = [], []
    for half, grad in zip(normed_second, last_full):
        hidden = dot(half, fc1_weight, (1, 0)) + unit_bias
        spread = 0.5 * (1.0 + lax.erf(hidden * (1.0 / math.sqrt(2.0))))
        active.append((hidden * spread).astype(BF))
        slope = jnp.exp(-0.5 * hidden * hidden) * (1.0 / math.sqrt(2.0 * math.pi))
        slope = spread + hidden * slope
        hidden_grad.append((dot(grad, fc2_weight, (1, 1)) * slope).astype(BF))
    begun, sent = scatter_begin(hidden_grad, fc1_weight, (1, 1))
    normed_grad = scatter_end(begun, sent)
    fc2_grad = sum(dot(one, two, (0, 0)) for one, two in zip(active, last_full))
    fc1_grad = sum(dot(one, two, (0, 0)) for one, two in zip(normed_second, hidden_grad))
    unit_grad = sum(jnp.sum(half.astype(F32), axis=0) for half in hidden_grad)
    fc_own = jnp.concatenate([fc1_grad[: D // 2], fc2_grad[:, : D // 2]], axis=0)
    fc_other = jnp.concatenate([fc1_grad[D // 2 :], fc2_grad[:, D // 2 :]], axis=0)
    fc_sum = image_sum(fc_own, after(fc_other.astype(BF), *sent))
    scale_second = jnp.sum(fc2_weight.astype(F32) * fc2_grad, axis=0) / scales[1]
    scale_second = scale_second + second_bias[0] * jnp.sum(upstream, axis=0)

    upstream = upstream + norm_pull(normed_grad, scaled_second, inverse_second, gains[1])
    first_grad = (upstream * scales[0]).astype(BF)
    vectors = [
        jnp.sum(normed_grad * scaled_second, axis=0),
        jnp.sum(normed_grad, axis=0),
        jnp.sum(upstream * branch_first, axis=0),
        scale_second,
    ]
    carried = jnp.concatenate([first_grad[:HALF], jnp.stack(vectors).astype(BF)], axis=0)
    carried = gather(jnp.pad(carried, ((0, spare - 4), (0, 0))))
    fc_sum = replica_gather(replica_scatter(after(fc_sum, first_grad)))
    real = jnp.arange(NY * ROWS)[:, None] % ROWS < HALF
    first_full = [jnp.where(real, half, jnp.zeros((), BF)) for half in carried]
    spares = [half.reshape(NY, ROWS, D)[:, HALF : HALF + 4].astype(F32) for half in carried]
    vectors = sum(jnp.sum(half, axis=0) for half in spares)
    bias_first = sum(jnp.sum(half.astype(F32), axis=0, keepdims=True) for half in first_full)
    bias_second = sum(jnp.sum(half.astype(F32), axis=0, keepdims=True) for half in last_full)
    vectors = jnp.concatenate([vectors, bias_first, bias_second], axis=0)

    mixture_grad = [dot(half, out_block, (1, 1)).astype(BF) for half in first_full]
    mixture_grad = jnp.concatenate(mixture_grad, axis=0)
    half_rows = NY * ROWS
    out_grad = dot(first_full[0], mixture[:half_rows], (0, 0))
    out_grad = out_grad + dot(first_full[1], mixture[half_rows:], (0, 0))
    active = [after(half, first_full[1]) for half in active]
    branch_second = scatter_end(*scatter_begin(active, fc2_weight, (1, 0))) + second_bias
    packed_grad = attend_pull(packed, mask, mixture_grad)
    packed_halves = packed_grad[:half_rows], packed_grad[half_rows:]
    begun, sent = scatter_begin(packed_halves, qkv_weight, (1, 1))
    sent = after(sent, fc_sum, branch_second)
    normed_grad = scatter_end(begun, sent)
    output = place_out(after(x + scales[1] * branch_second, *sent), home)

    qkv_grad = sum(dot(one, two, (0, 0)) for one, two in zip(normed_first, packed_halves))
    totals = jnp.sum(packed_grad.astype(F32), axis=0)
    wide_weight = qkv_weight.astype(F32)
    shift_part = jnp.sum(wide_weight * totals, axis=1)
    product = jnp.sum(wide_weight * qkv_grad, axis=1)
    gain_part = (product - shifts[0] * shift_part) / gains[0]
    late = jnp.concatenate([qkv_grad, out_grad], axis=1)
    head_grad = totals.reshape(3, 2, HD)
    head_grad = jnp.stack([head_grad[0], head_grad[2]], axis=1).reshape(2, 128)
    head_own, head_other = pick(head_grad)
    unit_own, unit_other = pick(unit_grad.reshape(2, 256))
    zeros = jnp.zeros((128,), F32)
    own = jnp.concatenate([unit_own, head_own, zeros])[None]
    other = jnp.concatenate([unit_other, head_other, zeros])[None]
    late_own = jnp.concatenate([late[: D // 2], vectors[:, : D // 2], own], axis=0)
    late_other = jnp.concatenate([late[D // 2 :], vectors[:, D // 2 :], other], axis=0)
    late = image_sum(late_own, after(late_other.astype(BF), *sent))
    final = column_sum(jnp.stack([gain_part, shift_part]))
    final = final[:, : D // 2] + swap(final[:, D // 2 :], "xh")
    late = jnp.concatenate([late, final, jnp.zeros((32 - 9, D // 2), F32)], axis=0)
    late = replica_scatter(late)
    late = replica_gather(after(late, normed_grad))
    input_grad = place_out(
        upstream + norm_pull(normed_grad, scaled_first, inverse_first, gains[0]), home
    )

    qkv_grad = late[: D // 2, :384].reshape(D // 2, 3, 2, HD).transpose(0, 2, 1, 3)
    out_grad = late[: D // 2, 384:].T
    vectors = late[D // 2 : D // 2 + 9]
    small = vectors[6]
    return (
        output,
        input_grad,
        qkv_grad.reshape(1, D // 2, 384),
        small[256:384].reshape(1, 1, 1, 1, -1),
        out_grad[None],
        fc_sum[None, : D // 2],
        small[:256].reshape(1, 1, 1, -1),
        fc_sum[None, D // 2 :],
        jnp.stack([vectors[7], vectors[0]])[None],
        jnp.stack([vectors[8], vectors[1]])[None],
        vectors[2:4][None],
        vectors[4:6][None],
    )


def solution(mesh):
    fine = Mesh(mesh.devices.reshape(NZ, 2, 2, NY, 2), ("z", "xl") + GROUP)
    tokens = P(("z", "xl", "y", "c"), "xh")
    tall = P(None, "xh", ("y", "c"))
    wide = P(None, ("y", "c"), "xh")
    head = P(None, ("y", "c"), "xh", None, None)
    unit = P(None, ("y", "c"), "xh", None)
    vector = P(None, None, "xh")
    return jax.shard_map(
        shards,
        mesh=fine,
        in_specs=(
            tokens,
            tall,
            head,
            wide,
            tall,
            unit,
            wide,
            vector,
            vector,
            vector,
            vector,
            tokens,
        ),
        out_specs=(
            tokens,
            tokens,
            tall,
            head,
            wide,
            tall,
            unit,
            wide,
            vector,
            vector,
            vector,
            vector,
        ),
        check_vma=False,
    )
```

```python
import math

import jax
import jax.numpy as jnp
from jax import lax
from jax.experimental import pallas as pl
from jax.experimental.pallas import tpu as pltpu
from jax.sharding import Mesh, PartitionSpec as P

D = 1024
HD = 64
SEQ = 1025
EPSILON = 1e-06
MASKED = -1000000000.0

HALF = 129
ROWS = 136
SLOTS = 8
NY = 4
NZ = 4

F32 = jnp.float32
BF = jnp.bfloat16
GROUP = ("xh", "y", "c")


def is_home(r, y):
    return y // 2 == r


def group_index(r, y, c):
    return (r * NY + y % NY) * 2 + c


def entry_pairs():
    places = [(r, y, c) for r in range(2) for y in range(NY) for c in range(2)]
    first, second = [], []
    for r, y, c in places:
        me = group_index(r, y, c)
        if is_home(r, y):
            first.append((me, group_index(r, y + 2, c)))
        else:
            first.append((me, group_index(1 - r, y, c)))
            second.append((me, group_index(1 - r, y + 2, c)))
    return first, second


ENTRY_FIRST, ENTRY_SECOND = entry_pairs()
EXIT_FIRST = [(b, a) for a, b in ENTRY_FIRST]
EXIT_SECOND = [(b, a) for a, b in ENTRY_SECOND]


def swap(value, axis):
    return lax.ppermute(value, axis, [(0, 1), (1, 0)])


def pull(value, axis, distance):
    return lax.ppermute(value, axis, [((i + distance) % 4, i) for i in range(4)])


def after(value, *earlier):
    return lax.optimization_barrier((value,) + earlier)[0]


def place_in(block, spare, home):
    first = jnp.concatenate([block[:HALF], spare], axis=0)
    second = jnp.concatenate([block[HALF:], spare], axis=0)
    moved = lax.ppermute(jnp.where(home, second, first), GROUP, ENTRY_FIRST)
    crossed = lax.ppermute(second, GROUP, ENTRY_SECOND)
    return jnp.where(home, first, moved), jnp.where(home, moved, crossed)


def place_out(values, home):
    own, other = values[:HALF, : D // 2], values[:HALF, D // 2 :].astype(BF)
    moved = lax.ppermute(jnp.where(home, other, own.astype(BF)), GROUP, EXIT_FIRST)
    crossed = lax.ppermute(other, GROUP, EXIT_SECOND)
    moved, crossed = moved.astype(F32), crossed.astype(F32)
    return jnp.concatenate([jnp.where(home, own, moved), jnp.where(home, moved, crossed)], axis=0)


def gather(piece):
    near = jnp.concatenate([piece] + [pull(piece, "y", d) for d in (1, 2, 3)], axis=0)
    return near, swap(near, "c")


def scatter_begin(halves, weight, contract):
    near, far = halves
    far = swap(dot(far, weight, contract).astype(BF), "c")
    summed = dot(near, weight, contract) + far.astype(F32)
    return summed[:ROWS], [summed[d * ROWS : (d + 1) * ROWS].astype(BF) for d in (1, 2, 3)]


def scatter_end(total, pieces):
    for d, piece in zip((1, 2, 3), pieces):
        total = total + pull(piece, "y", -d).astype(F32)
    return total


def image_sum(own, other):
    return own + swap(other.astype(BF), "xh").astype(F32)


def replica_scatter(values):
    rows = values.shape[0] // NZ
    z = lax.axis_index("z")

    def chunk(d):
        return lax.dynamic_slice_in_dim(values, ((z + d) % NZ) * rows, rows, 0)

    total = chunk(0)
    for d in (1, 2, 3):
        total = total + pull(chunk(d).astype(BF), "z", -d).astype(F32)
    return total.astype(BF)


def replica_gather(total):
    z = lax.axis_index("z")
    total = (total.astype(F32) + swap(total, "xl").astype(F32)).astype(BF)
    pieces = [total] + [pull(total, "z", d) for d in (1, 2, 3)]

    def slot(k):
        d = (k - z) % NZ
        low = jnp.where(d == 0, pieces[0], pieces[1])
        return jnp.where(d < 2, low, jnp.where(d == 2, pieces[2], pieces[3])).astype(F32)

    return jnp.concatenate([slot(k) for k in range(NZ)], axis=0)


def column_sum(values):
    values = values + swap(values, "c")
    opposite, later, earlier = (pull(values, "y", d) for d in (2, 1, 3))
    return (values + opposite) + (later + earlier)


def dot(first, second, contract):
    return lax.dot_general(
        first, second, (((contract[0],), (contract[1],)), ((), ())), preferred_element_type=F32
    )


def norm(values, gain, shift):
    center = jnp.mean(values, axis=1, keepdims=True)
    moved = values - center
    inverse = lax.rsqrt(jnp.mean(moved * moved, axis=1, keepdims=True) + EPSILON)
    scaled = moved * inverse
    return (scaled * gain + shift).astype(BF), scaled, inverse


def norm_pull(grad, scaled, inverse, gain):
    weighted = grad * gain
    mean = jnp.mean(weighted, axis=1, keepdims=True)
    inner = jnp.mean(weighted * scaled, axis=1, keepdims=True)
    return inverse * (weighted - mean - scaled * inner)


BLOCK = 272


def chances(query, key, mask):
    scores = dot(query * (1.0 / math.sqrt(HD)), key, (1, 1))
    scores = jnp.where(mask > 0, scores, MASKED)
    weights = jnp.exp(scores - jnp.max(scores, axis=1, keepdims=True))
    return weights * (1.0 / jnp.sum(weights, axis=1, keepdims=True))


def attend_kernel(mask_ref, packed_ref, out_ref):
    mask = mask_ref[...]
    for head in range(2):
        part = [slice(128 * s + HD * head, 128 * s + HD * (head + 1)) for s in range(3)]
        key, value = packed_ref[:, part[1]], packed_ref[:, part[2]]
        for block in range(SLOTS * ROWS // BLOCK):
            rows = slice(block * BLOCK, (block + 1) * BLOCK)
            chance = chances(packed_ref[rows, part[0]], key, mask).astype(BF)
            out_ref[rows, part[0]] = dot(chance, value, (1, 0)).astype(BF)


def attend_pull_kernel(mask_ref, packed_ref, grad_ref, out_ref):
    mask = mask_ref[...]
    factor = 1.0 / math.sqrt(HD)
    for head in range(2):
        part = [slice(128 * s + HD * head, 128 * s + HD * (head + 1)) for s in range(3)]
        key, value = packed_ref[:, part[1]], packed_ref[:, part[2]]
        key_grad = jnp.zeros((SLOTS * ROWS, HD), F32)
        value_grad = jnp.zeros((SLOTS * ROWS, HD), F32)
        for block in range(SLOTS * ROWS // BLOCK):
            rows = slice(block * BLOCK, (block + 1) * BLOCK)
            query, grad = packed_ref[rows, part[0]], grad_ref[rows, part[0]]
            chance = chances(query, key, mask)
            chance_grad = dot(grad, value, (1, 1))
            inner = jnp.sum(chance_grad * chance, axis=1, keepdims=True)
            score_grad = (chance * (chance_grad - inner)).astype(BF)
            out_ref[rows, part[0]] = (dot(score_grad, key, (1, 0)) * factor).astype(BF)
            key_grad = key_grad + dot(score_grad, query, (0, 0))
            value_grad = value_grad + dot(chance.astype(BF), grad, (0, 0))
        out_ref[:, part[1]] = (key_grad * factor).astype(BF)
        out_ref[:, part[2]] = value_grad.astype(BF)


def local_kernel(kernel, width, micros, *operands):
    return pl.pallas_call(
        kernel,
        out_shape=jax.ShapeDtypeStruct((SLOTS * ROWS, width), BF),
        in_specs=[pl.BlockSpec(memory_space=pltpu.VMEM)] * len(operands),
        out_specs=pl.BlockSpec(memory_space=pltpu.VMEM),
        compiler_params=pltpu.CompilerParams(vmem_limit_bytes=32 * 1024 * 1024),
        cost_estimate=pl.CostEstimate(
            flops=micros * 1000000000, bytes_accessed=micros * 3000000, transcendentals=0
        ),
    )(*operands)


def attend(packed, mask):
    return local_kernel(attend_kernel, 2 * HD, 8, mask, packed)


def attend_pull(packed, mask, mixture_grad):
    return local_kernel(attend_pull_kernel, 6 * HD, 12, mask, packed, mixture_grad)


def shards(
    inputs,
    w_qkv,
    qv_bias,
    w_out,
    w_fc1,
    fc1_bias,
    w_fc2,
    ln_gain,
    ln_bias,
    layer_scale,
    branch_bias,
    cotangent,
):
    r, y, c = (lax.axis_index(name) for name in GROUP)
    home = is_home(r, y)

    def in_order(mine, other):
        return jnp.where(r == 0, jnp.concatenate([mine, other]), jnp.concatenate([other, mine]))

    def pick(pair):
        return jnp.where(r == 0, pair[0], pair[1]), jnp.where(r == 0, pair[1], pair[0])

    own_rows = [ln_gain[0], ln_bias[0], layer_scale[0], branch_bias[0]]
    own_rows = jnp.concatenate(own_rows, axis=0)
    small = jnp.concatenate([qv_bias.reshape(-1), fc1_bias.reshape(-1)])
    spare = ROWS - HALF
    spare_rows = jnp.pad(own_rows[spare:], ((0, spare - 1), (0, 0)))
    spare_rows = jnp.concatenate([own_rows[:spare], spare_rows], axis=1)
    block = jnp.concatenate([inputs, cotangent], axis=1)
    mine, theirs = place_in(block, spare_rows, home)
    real = jnp.arange(ROWS)[:, None] < HALF
    x = jnp.concatenate([mine[:, : D // 2], theirs[:, : D // 2]], axis=1)
    x = jnp.where(real, x.astype(F32), 0.0)
    upstream = jnp.concatenate([mine[:, D // 2 :], theirs[:, D // 2 :]], axis=1)
    upstream = jnp.where(real, upstream.astype(F32), 0.0)
    rows = jnp.concatenate([own_rows[:spare], theirs[HALF:, : D // 2]], axis=1).astype(F32)
    gains, shifts, scales, first_bias = rows[0:2], rows[2:4], rows[4:6], rows[6:7]
    second_bias = theirs[HALF : HALF + 1, D // 2 :]
    second_bias = jnp.concatenate([own_rows[spare:], second_bias], axis=1).astype(F32)

    out_columns = w_out[0].reshape(128, 4, 128).transpose(1, 0, 2).reshape(D // 2, 128)
    first_weights = jnp.concatenate([w_qkv[0], out_columns], axis=1)
    small_row = jnp.pad(small[None], ((0, 15), (0, 128)))
    first_weights = jnp.concatenate([first_weights, small_row], axis=0)
    first_weights = swap(after(first_weights, theirs), "xh")
    small_other = first_weights[D // 2, :384]
    qkv_weight = jnp.concatenate([w_qkv[0], first_weights[: D // 2, :384]], axis=0)
    qkv_weight = qkv_weight.reshape(D, 2, 3, HD).transpose(0, 2, 1, 3).reshape(D, 6 * HD)
    out_other = first_weights[: D // 2, 384:].reshape(4, 128, 128).transpose(1, 0, 2)
    out_block = jnp.concatenate([w_out[0], out_other.reshape(128, D // 2)], axis=1)
    fc1_other = swap(after(w_fc1[0], first_weights), "xh")
    fc2_other = swap(after(w_fc2[0], fc1_other), "xh")
    fc1_weight = jnp.concatenate([w_fc1[0], fc1_other], axis=0)
    fc2_weight = jnp.concatenate([w_fc2[0], fc2_other], axis=1)
    normed, scaled_first, inverse_first = norm(x, gains[0], shifts[0])
    normed_first = gather(normed)
    head_bias = in_order(small[:128], small_other[:128]).astype(F32).reshape(2, 2, HD)
    zeros = jnp.zeros((128,), F32)
    full_bias = jnp.concatenate([head_bias[:, 0].reshape(-1), zeros, head_bias[:, 1].reshape(-1)])
    unit_bias = in_order(small[128:], small_other[128:]).astype(F32)

    packed = [(dot(half, qkv_weight, (1, 0)) + full_bias).astype(BF) for half in normed_first]
    packed = jnp.concatenate(packed, axis=0)
    position = jnp.arange(SLOTS * ROWS)
    slot, local = position // ROWS, position % ROWS
    owner_y, owner_c = (y + slot % NY) % NY, c ^ (slot // NY)
    last = (owner_y == (2 * r + 3) % NY) & (owner_c == 1)
    mask = local < jnp.where(last, HALF - (8 * HALF - SEQ), HALF)
    mask = mask.astype(F32)[None]
    last_grad = (upstream * scales[1]).astype(BF)
    last_full = gather(after(last_grad, normed_first[0]))
    mixture = attend(after(packed, fc1_other, last_full[0]), mask)
    half_rows = NY * ROWS
    mixture_halves = mixture[:half_rows], mixture[half_rows:]
    begun, sent = scatter_begin(mixture_halves, out_block, (1, 0))
    branch_first = scatter_end(begun, sent) + first_bias
    x = x + scales[0] * branch_first

    normed, scaled_second, inverse_second = norm(x, gains[1], shifts[1])
    normed_second = gather(after(normed, fc2_other, last_full[1]))
    active, hidden_grad = [], []
    for half, grad in zip(normed_second, last_full):
        hidden = dot(half, fc1_weight, (1, 0)) + unit_bias
        spread = 0.5 * (1.0 + lax.erf(hidden * (1.0 / math.sqrt(2.0))))
        active.append((hidden * spread).astype(BF))
        slope = jnp.exp(-0.5 * hidden * hidden) * (1.0 / math.sqrt(2.0 * math.pi))
        slope = spread + hidden * slope
        hidden_grad.append((dot(grad, fc2_weight, (1, 1)) * slope).astype(BF))
    begun, sent = scatter_begin(hidden_grad, fc1_weight, (1, 1))
    normed_grad = scatter_end(begun, sent)
    fc2_grad = sum(dot(one, two, (0, 0)) for one, two in zip(active, last_full))
    fc1_grad = sum(dot(one, two, (0, 0)) for one, two in zip(normed_second, hidden_grad))
    unit_grad = sum(jnp.sum(half.astype(F32), axis=0) for half in hidden_grad)
    fc2_sum = image_sum(fc2_grad[:, : D // 2], after(fc2_grad[:, D // 2 :].astype(BF), *sent))
    fc1_sum = image_sum(fc1_grad[: D // 2], after(fc1_grad[D // 2 :].astype(BF), fc2_sum))
    scale_second = jnp.sum(fc2_weight.astype(F32) * fc2_grad, axis=0) / scales[1]
    scale_second = scale_second + second_bias[0] * jnp.sum(upstream, axis=0)

    upstream = upstream + norm_pull(normed_grad, scaled_second, inverse_second, gains[1])
    first_grad = after((upstream * scales[0]).astype(BF), fc2_sum)
    vectors = [
        jnp.sum(normed_grad * scaled_second, axis=0),
        jnp.sum(normed_grad, axis=0),
        jnp.sum(upstream * branch_first, axis=0),
        scale_second,
    ]
    carried = jnp.concatenate([first_grad[:HALF], jnp.stack(vectors).astype(BF)], axis=0)
    carried = gather(jnp.pad(carried, ((0, spare - 4), (0, 0))))
    real = jnp.arange(NY * ROWS)[:, None] % ROWS < HALF
    first_full = [jnp.where(real, half, jnp.zeros((), BF)) for half in carried]
    spares = [half.reshape(NY, ROWS, D)[:, HALF : HALF + 4].astype(F32) for half in carried]
    vectors = sum(jnp.sum(half, axis=0) for half in spares)
    bias_first = sum(jnp.sum(half.astype(F32), axis=0, keepdims=True) for half in first_full)
    bias_second = sum(jnp.sum(half.astype(F32), axis=0, keepdims=True) for half in last_full)
    vectors = jnp.concatenate([vectors, bias_first, bias_second], axis=0)

    mixture_grad = [dot(half, out_block, (1, 1)).astype(BF) for half in first_full]
    fc_sum = jnp.concatenate([fc1_sum, fc2_sum], axis=0)
    mixture_grad = after(jnp.concatenate(mixture_grad, axis=0), fc_sum)
    out_grad = sum(dot(one, two, (0, 0)) for one, two in zip(first_full, mixture_halves))
    packed_grad = attend_pull(packed, mask, mixture_grad)
    packed_halves = packed_grad[:half_rows], packed_grad[half_rows:]
    begun, sent = scatter_begin(packed_halves, qkv_weight, (1, 1))
    arrived = [pull(piece, "y", -d) for d, piece in zip((1, 2, 3), sent)]
    normed_grad = begun + sum(piece.astype(F32) for piece in arrived)
    packed_grad = after(packed_grad, *sent)
    packed_halves = packed_grad[:half_rows], packed_grad[half_rows:]
    qkv_grad = sum(dot(one, two, (0, 0)) for one, two in zip(normed_first, packed_halves))
    totals = jnp.sum(packed_grad.astype(F32), axis=0)
    wide_weight = qkv_weight.astype(F32)
    shift_part = jnp.sum(wide_weight * totals, axis=1)
    product = jnp.sum(wide_weight * qkv_grad, axis=1)
    gain_part = (product - shifts[0] * shift_part) / gains[0]
    late = jnp.concatenate([qkv_grad, out_grad], axis=1)
    head_grad = totals.reshape(3, 2, HD)
    head_grad = jnp.stack([head_grad[0], head_grad[2]], axis=1).reshape(2, 128)
    head_own, head_other = pick(head_grad)
    unit_own, unit_other = pick(unit_grad.reshape(2, 256))
    zeros = jnp.zeros((128,), F32)
    own = jnp.concatenate([unit_own, head_own, zeros])[None]
    other = jnp.concatenate([unit_other, head_other, zeros])[None]
    late_own = jnp.concatenate([late[: D // 2], vectors[:, : D // 2], own], axis=0)
    late_other = jnp.concatenate([late[D // 2 :], vectors[:, D // 2 :], other], axis=0)
    late_other = late_other.astype(BF)
    late = image_sum(late_own, late_other)
    fc_sum = replica_gather(replica_scatter(after(fc_sum, arrived[0])))
    active = [after(half, late_other) for half in active]
    branch_second, pieces = scatter_begin(active, fc2_weight, (1, 0))
    normed_grad = after(normed_grad, *pieces)
    branch_second = scatter_end(branch_second, after(pieces, normed_grad)) + second_bias
    output = place_out(x + scales[1] * branch_second, home)
    final = column_sum(after(jnp.stack([gain_part, shift_part]), normed_grad))
    final = final[:, : D // 2] + swap(final[:, D // 2 :], "xh")
    late = jnp.concatenate([late, final, jnp.zeros((32 - 9, D // 2), F32)], axis=0)
    first_pull = norm_pull(normed_grad, scaled_first, inverse_first, gains[0])
    input_grad = place_out(upstream + first_pull, home)
    late = replica_gather(replica_scatter(after(late, fc_sum, branch_second, first_pull)))

    qkv_grad = late[: D // 2, :384].reshape(D // 2, 3, 2, HD).transpose(0, 2, 1, 3)
    out_grad = late[: D // 2, 384:].T
    vectors = late[D // 2 : D // 2 + 9]
    small = vectors[6]
    return (
        output,
        input_grad,
        qkv_grad.reshape(1, D // 2, 384),
        small[256:384].reshape(1, 1, 1, 1, -1),
        out_grad[None],
        fc_sum[None, : D // 2],
        small[:256].reshape(1, 1, 1, -1),
        fc_sum[None, D // 2 :],
        jnp.stack([vectors[7], vectors[0]])[None],
        jnp.stack([vectors[8], vectors[1]])[None],
        vectors[2:4][None],
        vectors[4:6][None],
    )


def solution(mesh):
    fine = Mesh(mesh.devices.reshape(NZ, 2, 2, NY, 2), ("z", "xl") + GROUP)
    tokens = P(("z", "xl", "y", "c"), "xh")
    tall = P(None, "xh", ("y", "c"))
    wide = P(None, ("y", "c"), "xh")
    head = P(None, ("y", "c"), "xh", None, None)
    unit = P(None, ("y", "c"), "xh", None)
    vector = P(None, None, "xh")
    return jax.shard_map(
        shards,
        mesh=fine,
        in_specs=(
            tokens,
            tall,
            head,
            wide,
            tall,
            unit,
            wide,
            vector,
            vector,
            vector,
            vector,
            tokens,
        ),
        out_specs=(
            tokens,
            tokens,
            tall,
            head,
            wide,
            tall,
            unit,
            wide,
            vector,
            vector,
            vector,
            vector,
        ),
        check_vma=False,
    )
```

```python
import math

import jax
import jax.numpy as jnp
from jax import lax
from jax.experimental import pallas as pl
from jax.experimental.pallas import tpu as pltpu
from jax.sharding import Mesh, PartitionSpec as P

D = 1024
HD = 64
SEQ = 1025
EPSILON = 1e-06
MASKED = -1000000000.0

HALF = 129
ROWS = 136
SLOTS = 8
NY = 4
NZ = 4

F32 = jnp.float32
BF = jnp.bfloat16
GROUP = ("xh", "y", "c")


def is_home(r, y):
    return y // 2 == r


def group_index(r, y, c):
    return (r * NY + y % NY) * 2 + c


def entry_pairs():
    places = [(r, y, c) for r in range(2) for y in range(NY) for c in range(2)]
    first, second = [], []
    for r, y, c in places:
        me = group_index(r, y, c)
        if is_home(r, y):
            first.append((me, group_index(r, y + 2, c)))
        else:
            first.append((me, group_index(1 - r, y, c)))
            second.append((me, group_index(1 - r, y + 2, c)))
    return first, second


ENTRY_FIRST, ENTRY_SECOND = entry_pairs()
EXIT_FIRST = [(b, a) for a, b in ENTRY_FIRST]
EXIT_SECOND = [(b, a) for a, b in ENTRY_SECOND]


def swap(value, axis):
    return lax.ppermute(value, axis, [(0, 1), (1, 0)])


def pull(value, axis, distance):
    return lax.ppermute(value, axis, [((i + distance) % 4, i) for i in range(4)])


def after(value, *earlier):
    return lax.optimization_barrier((value,) + earlier)[0]


def place_in(block, spare, home):
    first = jnp.concatenate([block[:HALF], spare], axis=0)
    second = jnp.concatenate([block[HALF:], spare], axis=0)
    moved = lax.ppermute(jnp.where(home, second, first), GROUP, ENTRY_FIRST)
    crossed = lax.ppermute(second, GROUP, ENTRY_SECOND)
    return jnp.where(home, first, moved), jnp.where(home, moved, crossed)


def place_out(values, home):
    own, other = values[:HALF, : D // 2], values[:HALF, D // 2 :].astype(BF)
    moved = lax.ppermute(jnp.where(home, other, own.astype(BF)), GROUP, EXIT_FIRST)
    crossed = lax.ppermute(other, GROUP, EXIT_SECOND)
    moved, crossed = moved.astype(F32), crossed.astype(F32)
    return jnp.concatenate([jnp.where(home, own, moved), jnp.where(home, moved, crossed)], axis=0)


def gather(piece):
    near = jnp.concatenate([piece] + [pull(piece, "y", d) for d in (1, 2, 3)], axis=0)
    return near, swap(near, "c")


def scatter_begin(halves, weight, contract):
    near, far = halves
    far = swap(dot(far, weight, contract).astype(BF), "c")
    summed = dot(near, weight, contract) + far.astype(F32)
    return summed[:ROWS], [summed[d * ROWS : (d + 1) * ROWS].astype(BF) for d in (1, 2, 3)]


def scatter_end(total, pieces):
    for d, piece in zip((1, 2, 3), pieces):
        total = total + pull(piece, "y", -d).astype(F32)
    return total


def image_sum(own, other):
    return own + swap(other.astype(BF), "xh").astype(F32)


def replica_scatter(arrays):
    z = lax.axis_index("z")

    def chunk(d):
        sizes = [values.shape[0] // NZ for values in arrays]
        cuts = [
            lax.dynamic_slice_in_dim(values, ((z + d) % NZ) * rows, rows, 0)
            for values, rows in zip(arrays, sizes)
        ]
        return jnp.concatenate(cuts, axis=0)

    total = chunk(0)
    for d in (1, 2, 3):
        total = total + pull(chunk(d).astype(BF), "z", -d).astype(F32)
    return total.astype(BF)


def replica_gather(total, split):
    z = lax.axis_index("z")
    total = (total.astype(F32) + swap(total, "xl").astype(F32)).astype(BF)
    pieces = [total] + [pull(total, "z", d) for d in (1, 2, 3)]

    def whole(parts):
        slots = []
        for k in range(NZ):
            d = (k - z) % NZ
            low = jnp.where(d == 0, parts[0], parts[1])
            high = jnp.where(d == 2, parts[2], parts[3])
            slots.append(jnp.where(d < 2, low, high).astype(F32))
        return jnp.concatenate(slots, axis=0)

    return whole([piece[:split] for piece in pieces]), whole([piece[split:] for piece in pieces])


def column_sum(values):
    values = values + swap(values, "c")
    opposite, later, earlier = (pull(values, "y", d) for d in (2, 1, 3))
    return (values + opposite) + (later + earlier)


def dot(first, second, contract):
    return lax.dot_general(
        first, second, (((contract[0],), (contract[1],)), ((), ())), preferred_element_type=F32
    )


def norm(values, gain, shift):
    center = jnp.mean(values, axis=1, keepdims=True)
    moved = values - center
    inverse = lax.rsqrt(jnp.mean(moved * moved, axis=1, keepdims=True) + EPSILON)
    scaled = moved * inverse
    return (scaled * gain + shift).astype(BF), scaled, inverse


def norm_pull(grad, scaled, inverse, gain):
    weighted = grad * gain
    mean = jnp.mean(weighted, axis=1, keepdims=True)
    inner = jnp.mean(weighted * scaled, axis=1, keepdims=True)
    return inverse * (weighted - mean - scaled * inner)


BLOCK = 272


def chances(query, key, mask):
    scores = dot(query * (1.0 / math.sqrt(HD)), key, (1, 1))
    scores = jnp.where(mask > 0, scores, MASKED)
    weights = jnp.exp(scores - jnp.max(scores, axis=1, keepdims=True))
    return weights * (1.0 / jnp.sum(weights, axis=1, keepdims=True))


def attend_kernel(mask_ref, packed_ref, out_ref):
    mask = mask_ref[...]
    for head in range(2):
        part = [slice(128 * s + HD * head, 128 * s + HD * (head + 1)) for s in range(3)]
        key, value = packed_ref[:, part[1]], packed_ref[:, part[2]]
        for block in range(SLOTS * ROWS // BLOCK):
            rows = slice(block * BLOCK, (block + 1) * BLOCK)
            chance = chances(packed_ref[rows, part[0]], key, mask).astype(BF)
            out_ref[rows, part[0]] = dot(chance, value, (1, 0)).astype(BF)


def attend_pull_kernel(mask_ref, packed_ref, grad_ref, out_ref):
    mask = mask_ref[...]
    factor = 1.0 / math.sqrt(HD)
    for head in range(2):
        part = [slice(128 * s + HD * head, 128 * s + HD * (head + 1)) for s in range(3)]
        key, value = packed_ref[:, part[1]], packed_ref[:, part[2]]
        key_grad = jnp.zeros((SLOTS * ROWS, HD), F32)
        value_grad = jnp.zeros((SLOTS * ROWS, HD), F32)
        for block in range(SLOTS * ROWS // BLOCK):
            rows = slice(block * BLOCK, (block + 1) * BLOCK)
            query, grad = packed_ref[rows, part[0]], grad_ref[rows, part[0]]
            chance = chances(query, key, mask)
            chance_grad = dot(grad, value, (1, 1))
            inner = jnp.sum(chance_grad * chance, axis=1, keepdims=True)
            score_grad = (chance * (chance_grad - inner)).astype(BF)
            out_ref[rows, part[0]] = (dot(score_grad, key, (1, 0)) * factor).astype(BF)
            key_grad = key_grad + dot(score_grad, query, (0, 0))
            value_grad = value_grad + dot(chance.astype(BF), grad, (0, 0))
        out_ref[:, part[1]] = (key_grad * factor).astype(BF)
        out_ref[:, part[2]] = value_grad.astype(BF)


def local_kernel(kernel, width, micros, *operands):
    return pl.pallas_call(
        kernel,
        out_shape=jax.ShapeDtypeStruct((SLOTS * ROWS, width), BF),
        in_specs=[pl.BlockSpec(memory_space=pltpu.VMEM)] * len(operands),
        out_specs=pl.BlockSpec(memory_space=pltpu.VMEM),
        compiler_params=pltpu.CompilerParams(vmem_limit_bytes=32 * 1024 * 1024),
        cost_estimate=pl.CostEstimate(
            flops=micros * 1000000000, bytes_accessed=micros * 3000000, transcendentals=0
        ),
    )(*operands)


def attend(packed, mask):
    return local_kernel(attend_kernel, 2 * HD, 8, mask, packed)


def attend_pull(packed, mask, mixture_grad):
    return local_kernel(attend_pull_kernel, 6 * HD, 12, mask, packed, mixture_grad)


def shards(
    inputs,
    w_qkv,
    qv_bias,
    w_out,
    w_fc1,
    fc1_bias,
    w_fc2,
    ln_gain,
    ln_bias,
    layer_scale,
    branch_bias,
    cotangent,
):
    r, y, c = (lax.axis_index(name) for name in GROUP)
    home = is_home(r, y)

    def in_order(mine, other):
        return jnp.where(r == 0, jnp.concatenate([mine, other]), jnp.concatenate([other, mine]))

    def pick(pair):
        return jnp.where(r == 0, pair[0], pair[1]), jnp.where(r == 0, pair[1], pair[0])

    own_rows = [ln_gain[0], ln_bias[0], layer_scale[0], branch_bias[0]]
    own_rows = jnp.concatenate(own_rows, axis=0)
    small = jnp.concatenate([qv_bias.reshape(-1), fc1_bias.reshape(-1)])
    spare = ROWS - HALF
    real = jnp.arange(ROWS)[:, None] < HALF
    mine, theirs = place_in(inputs, own_rows[:spare], home)
    x = jnp.where(real, jnp.concatenate([mine, theirs], axis=1).astype(F32), 0.0)
    rows = jnp.concatenate([own_rows[:spare], theirs[HALF:]], axis=1).astype(F32)
    gains, shifts, scales, first_bias = rows[0:2], rows[2:4], rows[4:6], rows[6:7]
    normed, scaled_first, inverse_first = norm(x, gains[0], shifts[0])
    normed_first = gather(normed)
    spare_rows = jnp.pad(own_rows[spare:], ((0, spare - 1), (0, 0)))
    mine, theirs = place_in(after(cotangent, normed), spare_rows, home)
    upstream = jnp.where(real, jnp.concatenate([mine, theirs], axis=1).astype(F32), 0.0)
    second_bias = theirs[HALF : HALF + 1]
    second_bias = jnp.concatenate([own_rows[spare:], second_bias], axis=1).astype(F32)

    out_columns = w_out[0].reshape(128, 4, 128).transpose(1, 0, 2).reshape(D // 2, 128)
    first_weights = jnp.concatenate([w_qkv[0], out_columns], axis=1)
    small_row = jnp.pad(small[None], ((0, 15), (0, 128)))
    first_weights = jnp.concatenate([first_weights, small_row], axis=0)
    first_weights = swap(after(first_weights, normed), "xh")
    small_other = first_weights[D // 2, :384]
    qkv_weight = jnp.concatenate([w_qkv[0], first_weights[: D // 2, :384]], axis=0)
    qkv_weight = qkv_weight.reshape(D, 2, 3, HD).transpose(0, 2, 1, 3).reshape(D, 6 * HD)
    out_other = first_weights[: D // 2, 384:].reshape(4, 128, 128).transpose(1, 0, 2)
    out_block = jnp.concatenate([w_out[0], out_other.reshape(128, D // 2)], axis=1)
    fc1_other = swap(after(w_fc1[0], first_weights), "xh")
    fc2_other = swap(after(w_fc2[0], fc1_other), "xh")
    fc1_weight = jnp.concatenate([w_fc1[0], fc1_other], axis=0)
    fc2_weight = jnp.concatenate([w_fc2[0], fc2_other], axis=1)
    head_bias = in_order(small[:128], small_other[:128]).astype(F32).reshape(2, 2, HD)
    zeros = jnp.zeros((128,), F32)
    full_bias = jnp.concatenate([head_bias[:, 0].reshape(-1), zeros, head_bias[:, 1].reshape(-1)])
    unit_bias = in_order(small[128:], small_other[128:]).astype(F32)

    packed = [(dot(half, qkv_weight, (1, 0)) + full_bias).astype(BF) for half in normed_first]
    packed = jnp.concatenate(packed, axis=0)
    position = jnp.arange(SLOTS * ROWS)
    slot, local = position // ROWS, position % ROWS
    owner_y, owner_c = (y + slot % NY) % NY, c ^ (slot // NY)
    last = (owner_y == (2 * r + 3) % NY) & (owner_c == 1)
    mask = local < jnp.where(last, HALF - (8 * HALF - SEQ), HALF)
    mask = mask.astype(F32)[None]
    last_grad = (upstream * scales[1]).astype(BF)
    last_full = gather(after(last_grad, normed_first[0]))
    mixture = attend(after(packed, fc1_other, last_full[0]), mask)
    half_rows = NY * ROWS
    mixture_halves = mixture[:half_rows], mixture[half_rows:]
    begun, sent = scatter_begin(mixture_halves, out_block, (1, 0))
    branch_first = scatter_end(begun, sent) + first_bias
    x = x + scales[0] * branch_first

    normed, scaled_second, inverse_second = norm(x, gains[1], shifts[1])
    normed_second = gather(after(normed, fc2_other, last_full[1]))
    active, hidden_grad = [], []
    for half, grad in zip(normed_second, last_full):
        hidden = dot(half, fc1_weight, (1, 0)) + unit_bias
        spread = 0.5 * (1.0 + lax.erf(hidden * (1.0 / math.sqrt(2.0))))
        active.append((hidden * spread).astype(BF))
        slope = jnp.exp(-0.5 * hidden * hidden) * (1.0 / math.sqrt(2.0 * math.pi))
        slope = spread + hidden * slope
        hidden_grad.append((dot(grad, fc2_weight, (1, 1)) * slope).astype(BF))
    begun, sent = scatter_begin(hidden_grad, fc1_weight, (1, 1))
    normed_grad = scatter_end(begun, sent)
    fc2_grad = sum(dot(one, two, (0, 0)) for one, two in zip(active, last_full))
    fc1_grad = sum(dot(one, two, (0, 0)) for one, two in zip(normed_second, hidden_grad))
    unit_grad = sum(jnp.sum(half.astype(F32), axis=0) for half in hidden_grad)
    fc2_sum = image_sum(fc2_grad[:, : D // 2], after(fc2_grad[:, D // 2 :].astype(BF), *sent))
    fc1_sum = image_sum(fc1_grad[: D // 2], after(fc1_grad[D // 2 :].astype(BF), fc2_sum))
    scale_second = jnp.sum(fc2_weight.astype(F32) * fc2_grad, axis=0) / scales[1]
    scale_second = scale_second + second_bias[0] * jnp.sum(upstream, axis=0)

    upstream = upstream + norm_pull(normed_grad, scaled_second, inverse_second, gains[1])
    first_grad = after((upstream * scales[0]).astype(BF), fc2_sum)
    vectors = [
        jnp.sum(normed_grad * scaled_second, axis=0),
        jnp.sum(normed_grad, axis=0),
        jnp.sum(upstream * branch_first, axis=0),
        scale_second,
    ]
    carried = jnp.concatenate([first_grad[:HALF], jnp.stack(vectors).astype(BF)], axis=0)
    carried = gather(jnp.pad(carried, ((0, spare - 4), (0, 0))))
    real = jnp.arange(NY * ROWS)[:, None] % ROWS < HALF
    first_full = [jnp.where(real, half, jnp.zeros((), BF)) for half in carried]
    spares = [half.reshape(NY, ROWS, D)[:, HALF : HALF + 4].astype(F32) for half in carried]
    vectors = sum(jnp.sum(half, axis=0) for half in spares)
    bias_first = sum(jnp.sum(half.astype(F32), axis=0, keepdims=True) for half in first_full)
    bias_second = sum(jnp.sum(half.astype(F32), axis=0, keepdims=True) for half in last_full)
    vectors = jnp.concatenate([vectors, bias_first, bias_second], axis=0)

    mixture_grad = [dot(half, out_block, (1, 1)).astype(BF) for half in first_full]
    fc_sum = jnp.concatenate([fc1_sum, fc2_sum], axis=0)
    mixture_grad = after(jnp.concatenate(mixture_grad, axis=0), fc_sum)
    out_grad = sum(dot(one, two, (0, 0)) for one, two in zip(first_full, mixture_halves))
    packed_grad = attend_pull(packed, mask, mixture_grad)
    packed_halves = packed_grad[:half_rows], packed_grad[half_rows:]
    begun, sent = scatter_begin(packed_halves, qkv_weight, (1, 1))
    arrived = [pull(piece, "y", -d) for d, piece in zip((1, 2, 3), sent)]
    normed_grad = begun + sum(piece.astype(F32) for piece in arrived)
    packed_grad = after(packed_grad, *sent)
    packed_halves = packed_grad[:half_rows], packed_grad[half_rows:]
    qkv_grad = sum(dot(one, two, (0, 0)) for one, two in zip(normed_first, packed_halves))
    totals = jnp.sum(packed_grad.astype(F32), axis=0)
    wide_weight = qkv_weight.astype(F32)
    shift_part = jnp.sum(wide_weight * totals, axis=1)
    product = jnp.sum(wide_weight * qkv_grad, axis=1)
    gain_part = (product - shifts[0] * shift_part) / gains[0]
    late = jnp.concatenate([qkv_grad, out_grad], axis=1)
    head_grad = totals.reshape(3, 2, HD)
    head_grad = jnp.stack([head_grad[0], head_grad[2]], axis=1).reshape(2, 128)
    head_own, head_other = pick(head_grad)
    unit_own, unit_other = pick(unit_grad.reshape(2, 256))
    zeros = jnp.zeros((128,), F32)
    own = jnp.concatenate([unit_own, head_own, zeros])[None]
    other = jnp.concatenate([unit_other, head_other, zeros])[None]
    late_own = jnp.concatenate([late[: D // 2], vectors[:, : D // 2], own], axis=0)
    late_other = jnp.concatenate([late[D // 2 :], vectors[:, D // 2 :], other], axis=0)
    late_other = late_other.astype(BF)
    late = image_sum(late_own, late_other)
    active = [after(half, late_other) for half in active]
    branch_second, pieces = scatter_begin(active, fc2_weight, (1, 0))
    normed_grad = after(normed_grad, *pieces)
    branch_second = scatter_end(branch_second, after(pieces, normed_grad)) + second_bias
    output = place_out(x + scales[1] * branch_second, home)
    final = column_sum(after(jnp.stack([gain_part, shift_part]), late_other, arrived[1]))
    final = final[:, : D // 2] + swap(final[:, D // 2 :], "xh")
    late = jnp.concatenate([late, final, jnp.zeros((32 - 9, D // 2), F32)], axis=0)
    first_pull = norm_pull(normed_grad, scaled_first, inverse_first, gains[0])
    input_grad = place_out(upstream + first_pull, home)
    quarter = replica_scatter([fc_sum, after(late, normed_grad)])
    quarter = after(quarter, branch_second, first_pull)
    fc_sum, late = replica_gather(quarter, fc_sum.shape[0] // NZ)

    qkv_grad = late[: D // 2, :384].reshape(D // 2, 3, 2, HD).transpose(0, 2, 1, 3)
    out_grad = late[: D // 2, 384:].T
    vectors = late[D // 2 : D // 2 + 9]
    small = vectors[6]
    return (
        output,
        input_grad,
        qkv_grad.reshape(1, D // 2, 384),
        small[256:384].reshape(1, 1, 1, 1, -1),
        out_grad[None],
        fc_sum[None, : D // 2],
        small[:256].reshape(1, 1, 1, -1),
        fc_sum[None, D // 2 :],
        jnp.stack([vectors[7], vectors[0]])[None],
        jnp.stack([vectors[8], vectors[1]])[None],
        vectors[2:4][None],
        vectors[4:6][None],
    )


def solution(mesh):
    fine = Mesh(mesh.devices.reshape(NZ, 2, 2, NY, 2), ("z", "xl") + GROUP)
    tokens = P(("z", "xl", "y", "c"), "xh")
    tall = P(None, "xh", ("y", "c"))
    wide = P(None, ("y", "c"), "xh")
    head = P(None, ("y", "c"), "xh", None, None)
    unit = P(None, ("y", "c"), "xh", None)
    vector = P(None, None, "xh")
    return jax.shard_map(
        shards,
        mesh=fine,
        in_specs=(
            tokens,
            tall,
            head,
            wide,
            tall,
            unit,
            wide,
            vector,
            vector,
            vector,
            vector,
            tokens,
        ),
        out_specs=(
            tokens,
            tokens,
            tall,
            head,
            wide,
            tall,
            unit,
            wide,
            vector,
            vector,
            vector,
            vector,
        ),
        check_vma=False,
    )
```

```python
import math

import jax
import jax.numpy as jnp
from jax import lax
from jax.experimental import pallas as pl
from jax.experimental.pallas import tpu as pltpu
from jax.sharding import Mesh, PartitionSpec as P

D = 1024
HD = 64
SEQ = 1025
EPSILON = 1e-06
MASKED = -1000000000.0

HALF = 129
ROWS = 136
SLOTS = 8
NY = 4
NZ = 4

F32 = jnp.float32
BF = jnp.bfloat16
GROUP = ("xh", "y", "c")


def is_home(r, y):
    return y // 2 == r


def group_index(r, y, c):
    return (r * NY + y % NY) * 2 + c


def entry_pairs():
    places = [(r, y, c) for r in range(2) for y in range(NY) for c in range(2)]
    first, second = [], []
    for r, y, c in places:
        me = group_index(r, y, c)
        if is_home(r, y):
            first.append((me, group_index(r, y + 2, c)))
        else:
            first.append((me, group_index(1 - r, y, c)))
            second.append((me, group_index(1 - r, y + 2, c)))
    return first, second


ENTRY_FIRST, ENTRY_SECOND = entry_pairs()
EXIT_FIRST = [(b, a) for a, b in ENTRY_FIRST]
EXIT_SECOND = [(b, a) for a, b in ENTRY_SECOND]


def swap(value, axis):
    return lax.ppermute(value, axis, [(0, 1), (1, 0)])


def pull(value, axis, distance):
    return lax.ppermute(value, axis, [((i + distance) % 4, i) for i in range(4)])


def after(value, *earlier):
    return lax.optimization_barrier((value,) + earlier)[0]


def place_in(block, spare, home):
    first = jnp.concatenate([block[:HALF], spare], axis=0)
    second = jnp.concatenate([block[HALF:], spare], axis=0)
    moved = lax.ppermute(jnp.where(home, second, first), GROUP, ENTRY_FIRST)
    crossed = lax.ppermute(second, GROUP, ENTRY_SECOND)
    return jnp.where(home, first, moved), jnp.where(home, moved, crossed)


def place_out(values, home):
    own, other = values[:HALF, : D // 2], values[:HALF, D // 2 :].astype(BF)
    moved = lax.ppermute(jnp.where(home, other, own.astype(BF)), GROUP, EXIT_FIRST)
    crossed = lax.ppermute(other, GROUP, EXIT_SECOND)
    moved, crossed = moved.astype(F32), crossed.astype(F32)
    return jnp.concatenate([jnp.where(home, own, moved), jnp.where(home, moved, crossed)], axis=0)


def gather(piece, *beside):
    near = jnp.concatenate([piece] + [pull(piece, "y", d) for d in (1, 2, 3)], axis=0)
    near = after(near, *beside)
    return near, swap(near, "c")


def scatter_begin(halves, weight, contract, extra=None):
    def product(half):
        result = dot(half, weight, contract)
        if extra is not None:
            row = jnp.arange(NY * ROWS)[:, None] % ROWS - HALF
            for i in range(extra.shape[0]):
                result = jnp.where(row == i, extra[i], result)
        return result

    near, far = halves
    far = swap(product(far).astype(BF), "c")
    summed = product(near) + far.astype(F32)
    return summed[:ROWS], [summed[d * ROWS : (d + 1) * ROWS].astype(BF) for d in (1, 2, 3)]


def scatter_end(total, pieces):
    for d, piece in zip((1, 2, 3), pieces):
        total = total + pull(piece, "y", -d).astype(F32)
    return total


def image_sum(own, other):
    return own + swap(other.astype(BF), "xh").astype(F32)


def replica_scatter(arrays):
    z = lax.axis_index("z")

    def chunk(d):
        sizes = [values.shape[0] // NZ for values in arrays]
        cuts = [
            lax.dynamic_slice_in_dim(values, ((z + d) % NZ) * rows, rows, 0)
            for values, rows in zip(arrays, sizes)
        ]
        return jnp.concatenate(cuts, axis=0)

    total = chunk(0)
    for d in (1, 2, 3):
        total = total + pull(chunk(d).astype(BF), "z", -d).astype(F32)
    return total.astype(BF)


def replica_gather(total, split):
    z = lax.axis_index("z")
    total = (total.astype(F32) + swap(total, "xl").astype(F32)).astype(BF)
    pieces = [total] + [pull(total, "z", d) for d in (1, 2, 3)]

    def whole(parts):
        slots = []
        for k in range(NZ):
            d = (k - z) % NZ
            low = jnp.where(d == 0, parts[0], parts[1])
            high = jnp.where(d == 2, parts[2], parts[3])
            slots.append(jnp.where(d < 2, low, high).astype(F32))
        return jnp.concatenate(slots, axis=0)

    return whole([piece[:split] for piece in pieces]), whole([piece[split:] for piece in pieces])


def dot(first, second, contract):
    return lax.dot_general(
        first, second, (((contract[0],), (contract[1],)), ((), ())), preferred_element_type=F32
    )


def norm(values, gain, shift):
    center = jnp.mean(values, axis=1, keepdims=True)
    moved = values - center
    inverse = lax.rsqrt(jnp.mean(moved * moved, axis=1, keepdims=True) + EPSILON)
    scaled = moved * inverse
    return (scaled * gain + shift).astype(BF), scaled, inverse


def norm_pull(grad, scaled, inverse, gain):
    weighted = grad * gain
    mean = jnp.mean(weighted, axis=1, keepdims=True)
    inner = jnp.mean(weighted * scaled, axis=1, keepdims=True)
    return inverse * (weighted - mean - scaled * inner)


BLOCK = 272


def chances(query, key, mask):
    scores = dot(query * (1.0 / math.sqrt(HD)), key, (1, 1))
    scores = jnp.where(mask > 0, scores, MASKED)
    weights = jnp.exp(scores - jnp.max(scores, axis=1, keepdims=True))
    return weights * (1.0 / jnp.sum(weights, axis=1, keepdims=True))


def attend_kernel(mask_ref, packed_ref, out_ref):
    mask = mask_ref[...]
    for head in range(2):
        part = [slice(128 * s + HD * head, 128 * s + HD * (head + 1)) for s in range(3)]
        key, value = packed_ref[:, part[1]], packed_ref[:, part[2]]
        for block in range(SLOTS * ROWS // BLOCK):
            rows = slice(block * BLOCK, (block + 1) * BLOCK)
            chance = chances(packed_ref[rows, part[0]], key, mask).astype(BF)
            out_ref[rows, part[0]] = dot(chance, value, (1, 0)).astype(BF)


def attend_pull_kernel(mask_ref, packed_ref, grad_ref, out_ref):
    mask = mask_ref[...]
    factor = 1.0 / math.sqrt(HD)
    for head in range(2):
        part = [slice(128 * s + HD * head, 128 * s + HD * (head + 1)) for s in range(3)]
        key, value = packed_ref[:, part[1]], packed_ref[:, part[2]]
        key_grad = jnp.zeros((SLOTS * ROWS, HD), F32)
        value_grad = jnp.zeros((SLOTS * ROWS, HD), F32)
        for block in range(SLOTS * ROWS // BLOCK):
            rows = slice(block * BLOCK, (block + 1) * BLOCK)
            query, grad = packed_ref[rows, part[0]], grad_ref[rows, part[0]]
            chance = chances(query, key, mask)
            chance_grad = dot(grad, value, (1, 1))
            inner = jnp.sum(chance_grad * chance, axis=1, keepdims=True)
            score_grad = (chance * (chance_grad - inner)).astype(BF)
            out_ref[rows, part[0]] = (dot(score_grad, key, (1, 0)) * factor).astype(BF)
            key_grad = key_grad + dot(score_grad, query, (0, 0))
            value_grad = value_grad + dot(chance.astype(BF), grad, (0, 0))
        out_ref[:, part[1]] = (key_grad * factor).astype(BF)
        out_ref[:, part[2]] = value_grad.astype(BF)


def local_kernel(kernel, width, micros, *operands):
    return pl.pallas_call(
        kernel,
        out_shape=jax.ShapeDtypeStruct((SLOTS * ROWS, width), BF),
        in_specs=[pl.BlockSpec(memory_space=pltpu.VMEM)] * len(operands),
        out_specs=pl.BlockSpec(memory_space=pltpu.VMEM),
        compiler_params=pltpu.CompilerParams(vmem_limit_bytes=32 * 1024 * 1024),
        cost_estimate=pl.CostEstimate(
            flops=micros * 1000000000, bytes_accessed=micros * 3000000, transcendentals=0
        ),
    )(*operands)


def attend(packed, mask):
    return local_kernel(attend_kernel, 2 * HD, 8, mask, packed)


def attend_pull(packed, mask, mixture_grad):
    return local_kernel(attend_pull_kernel, 6 * HD, 12, mask, packed, mixture_grad)


def shards(
    inputs,
    w_qkv,
    qv_bias,
    w_out,
    w_fc1,
    fc1_bias,
    w_fc2,
    ln_gain,
    ln_bias,
    layer_scale,
    branch_bias,
    cotangent,
):
    r, y, c = (lax.axis_index(name) for name in GROUP)
    home = is_home(r, y)

    def in_order(mine, other):
        return jnp.where(r == 0, jnp.concatenate([mine, other]), jnp.concatenate([other, mine]))

    def pick(pair):
        return jnp.where(r == 0, pair[0], pair[1]), jnp.where(r == 0, pair[1], pair[0])

    own_rows = [ln_gain[0], ln_bias[0], layer_scale[0], branch_bias[0]]
    own_rows = jnp.concatenate(own_rows, axis=0)
    small = jnp.concatenate([qv_bias.reshape(-1), fc1_bias.reshape(-1)])
    spare = ROWS - HALF
    real = jnp.arange(ROWS)[:, None] < HALF
    mine, theirs = place_in(inputs, own_rows[:spare], home)
    x = jnp.where(real, jnp.concatenate([mine, theirs], axis=1).astype(F32), 0.0)
    rows = jnp.concatenate([own_rows[:spare], theirs[HALF:]], axis=1).astype(F32)
    gains, shifts, scales, first_bias = rows[0:2], rows[2:4], rows[4:6], rows[6:7]
    normed, scaled_first, inverse_first = norm(x, gains[0], shifts[0])
    normed_first = gather(normed)
    spare_rows = jnp.pad(own_rows[spare:], ((0, spare - 1), (0, 0)))
    mine, theirs = place_in(after(cotangent, normed_first[0]), spare_rows, home)
    upstream = jnp.where(real, jnp.concatenate([mine, theirs], axis=1).astype(F32), 0.0)
    second_bias = theirs[HALF : HALF + 1]
    second_bias = jnp.concatenate([own_rows[spare:], second_bias], axis=1).astype(F32)

    out_columns = w_out[0].reshape(128, 4, 128).transpose(1, 0, 2).reshape(D // 2, 128)
    first_weights = jnp.concatenate([w_qkv[0], out_columns], axis=1)
    small_row = jnp.pad(small[None], ((0, 15), (0, 128)))
    first_weights = jnp.concatenate([first_weights, small_row], axis=0)
    first_weights = swap(after(first_weights, normed), "xh")
    small_other = first_weights[D // 2, :384]
    qkv_weight = jnp.concatenate([w_qkv[0], first_weights[: D // 2, :384]], axis=0)
    qkv_weight = qkv_weight.reshape(D, 2, 3, HD).transpose(0, 2, 1, 3).reshape(D, 6 * HD)
    out_other = first_weights[: D // 2, 384:].reshape(4, 128, 128).transpose(1, 0, 2)
    out_block = jnp.concatenate([w_out[0], out_other.reshape(128, D // 2)], axis=1)
    fc1_other = swap(after(w_fc1[0], first_weights), "xh")
    fc2_other = swap(after(w_fc2[0], fc1_other), "xh")
    fc1_weight = jnp.concatenate([w_fc1[0], fc1_other], axis=0)
    fc2_weight = jnp.concatenate([w_fc2[0], fc2_other], axis=1)
    head_bias = in_order(small[:128], small_other[:128]).astype(F32).reshape(2, 2, HD)
    zeros = jnp.zeros((128,), F32)
    full_bias = jnp.concatenate([head_bias[:, 0].reshape(-1), zeros, head_bias[:, 1].reshape(-1)])
    unit_bias = in_order(small[128:], small_other[128:]).astype(F32)

    packed = [(dot(half, qkv_weight, (1, 0)) + full_bias).astype(BF) for half in normed_first]
    packed = jnp.concatenate(packed, axis=0)
    position = jnp.arange(SLOTS * ROWS)
    slot, local = position // ROWS, position % ROWS
    owner_y, owner_c = (y + slot % NY) % NY, c ^ (slot // NY)
    last = (owner_y == (2 * r + 3) % NY) & (owner_c == 1)
    mask = local < jnp.where(last, HALF - (8 * HALF - SEQ), HALF)
    mask = mask.astype(F32)[None]
    last_grad = (upstream * scales[1]).astype(BF)
    last_full = gather(after(last_grad, normed_first[0]))
    mixture = attend(after(packed, fc1_other, last_full[0]), mask)
    half_rows = NY * ROWS
    mixture_halves = mixture[:half_rows], mixture[half_rows:]
    begun, sent = scatter_begin(mixture_halves, out_block, (1, 0))
    branch_first = scatter_end(begun, sent) + first_bias
    x = x + scales[0] * branch_first

    normed, scaled_second, inverse_second = norm(x, gains[1], shifts[1])
    normed_second = gather(after(normed, fc2_other, last_full[1]))
    active, hidden_grad = [], []
    for half, grad in zip(normed_second, last_full):
        hidden = dot(half, fc1_weight, (1, 0)) + unit_bias
        spread = 0.5 * (1.0 + lax.erf(hidden * (1.0 / math.sqrt(2.0))))
        active.append((hidden * spread).astype(BF))
        slope = jnp.exp(-0.5 * hidden * hidden) * (1.0 / math.sqrt(2.0 * math.pi))
        slope = spread + hidden * slope
        hidden_grad.append((dot(grad, fc2_weight, (1, 1)) * slope).astype(BF))
    begun, sent = scatter_begin(hidden_grad, fc1_weight, (1, 1))
    normed_grad = scatter_end(begun, sent)
    fc2_grad = sum(dot(one, two, (0, 0)) for one, two in zip(active, last_full))
    fc1_grad = sum(dot(one, two, (0, 0)) for one, two in zip(normed_second, hidden_grad))
    unit_grad = sum(jnp.sum(half.astype(F32), axis=0) for half in hidden_grad)
    fc2_sum = image_sum(fc2_grad[:, : D // 2], after(fc2_grad[:, D // 2 :].astype(BF), *sent))
    fc1_sum = image_sum(fc1_grad[: D // 2], after(fc1_grad[D // 2 :].astype(BF), fc2_sum))
    scale_second = jnp.sum(fc2_weight.astype(F32) * fc2_grad, axis=0) / scales[1]
    scale_second = scale_second + second_bias[0] * jnp.sum(upstream, axis=0)

    upstream = upstream + norm_pull(normed_grad, scaled_second, inverse_second, gains[1])
    first_grad = after((upstream * scales[0]).astype(BF), fc2_sum)
    vectors = [
        jnp.sum(normed_grad * scaled_second, axis=0),
        jnp.sum(normed_grad, axis=0),
        jnp.sum(upstream * branch_first, axis=0),
        scale_second,
    ]
    carried = jnp.concatenate([first_grad[:HALF], jnp.stack(vectors).astype(BF)], axis=0)
    carried = gather(jnp.pad(carried, ((0, spare - 4), (0, 0))), fc1_sum)
    real = jnp.arange(NY * ROWS)[:, None] % ROWS < HALF
    first_full = [jnp.where(real, half, jnp.zeros((), BF)) for half in carried]
    spares = [half.reshape(NY, ROWS, D)[:, HALF : HALF + 4].astype(F32) for half in carried]
    vectors = sum(jnp.sum(half, axis=0) for half in spares)
    bias_first = sum(jnp.sum(half.astype(F32), axis=0, keepdims=True) for half in first_full)
    bias_second = sum(jnp.sum(half.astype(F32), axis=0, keepdims=True) for half in last_full)
    vectors = jnp.concatenate([vectors, bias_first, bias_second], axis=0)

    mixture_grad = [dot(half, out_block, (1, 1)).astype(BF) for half in first_full]
    fc_sum = jnp.concatenate([fc1_sum, fc2_sum], axis=0)
    mixture_grad = jnp.concatenate(mixture_grad, axis=0)
    out_grad = sum(dot(one, two, (0, 0)) for one, two in zip(first_full, mixture_halves))
    packed_grad = attend_pull(packed, mask, mixture_grad)
    packed_halves = packed_grad[:half_rows], packed_grad[half_rows:]
    qkv_grad = sum(dot(one, two, (0, 0)) for one, two in zip(normed_first, packed_halves))
    totals = jnp.sum(packed_grad.astype(F32), axis=0)
    wide_weight = qkv_weight.astype(F32)
    shift_part = jnp.sum(wide_weight * totals, axis=1)
    product = jnp.sum(wide_weight * qkv_grad, axis=1)
    gain_part = (product - shifts[0] * shift_part) / gains[0]
    late = jnp.concatenate([qkv_grad, out_grad], axis=1)
    head_grad = totals.reshape(3, 2, HD)
    head_grad = jnp.stack([head_grad[0], head_grad[2]], axis=1).reshape(2, 128)
    head_own, head_other = pick(head_grad)
    unit_own, unit_other = pick(unit_grad.reshape(2, 256))
    zeros = jnp.zeros((128,), F32)
    own = jnp.concatenate([unit_own, head_own, zeros])[None]
    other = jnp.concatenate([unit_other, head_other, zeros])[None]
    late_own = jnp.concatenate([late[: D // 2], vectors[:, : D // 2], own], axis=0)
    late_other = jnp.concatenate([late[D // 2 :], vectors[:, D // 2 :], other], axis=0)
    late_other = late_other.astype(BF)
    late = image_sum(late_own, late_other)

    final = jnp.stack([gain_part, shift_part])
    packed_halves = after(packed_halves, late_other)
    begun, sent = scatter_begin(packed_halves, qkv_weight, (1, 1), final)
    normed_grad = scatter_end(begun, sent)
    final = normed_grad[HALF : HALF + 2]
    final = final[:, : D // 2] + swap(final[:, D // 2 :], "xh")
    late = jnp.concatenate([late, final, jnp.zeros((32 - 9, D // 2), F32)], axis=0)
    active = [after(half, normed_grad) for half in active]
    begun, sent = scatter_begin(active, fc2_weight, (1, 0))
    branch_second = scatter_end(begun, after(sent, late)) + second_bias
    output = place_out(x + scales[1] * branch_second, home)
    first_pull = norm_pull(normed_grad, scaled_first, inverse_first, gains[0])
    input_grad = place_out(upstream + first_pull, home)
    quarter = replica_scatter([fc_sum, late])
    quarter = after(quarter, branch_second, first_pull)
    fc_sum, late = replica_gather(quarter, fc_sum.shape[0] // NZ)

    qkv_grad = late[: D // 2, :384].reshape(D // 2, 3, 2, HD).transpose(0, 2, 1, 3)
    out_grad = late[: D // 2, 384:].T
    vectors, final = late[D // 2 : D // 2 + 7], late[D // 2 + 7 : D // 2 + 9]
    small = vectors[6]
    return (
        output,
        input_grad,
        qkv_grad.reshape(1, D // 2, 384),
        small[256:384].reshape(1, 1, 1, 1, -1),
        out_grad[None],
        fc_sum[None, : D // 2],
        small[:256].reshape(1, 1, 1, -1),
        fc_sum[None, D // 2 :],
        jnp.stack([final[0], vectors[0]])[None],
        jnp.stack([final[1], vectors[1]])[None],
        vectors[2:4][None],
        vectors[4:6][None],
    )


def solution(mesh):
    fine = Mesh(mesh.devices.reshape(NZ, 2, 2, NY, 2), ("z", "xl") + GROUP)
    tokens = P(("z", "xl", "y", "c"), "xh")
    tall = P(None, "xh", ("y", "c"))
    wide = P(None, ("y", "c"), "xh")
    head = P(None, ("y", "c"), "xh", None, None)
    unit = P(None, ("y", "c"), "xh", None)
    vector = P(None, None, "xh")
    return jax.shard_map(
        shards,
        mesh=fine,
        in_specs=(
            tokens,
            tall,
            head,
            wide,
            tall,
            unit,
            wide,
            vector,
            vector,
            vector,
            vector,
            tokens,
        ),
        out_specs=(
            tokens,
            tokens,
            tall,
            head,
            wide,
            tall,
            unit,
            wide,
            vector,
            vector,
            vector,
            vector,
        ),
        check_vma=False,
    )
```

```python
import math

import jax
import jax.numpy as jnp
from jax import lax
from jax.experimental import pallas as pl
from jax.experimental.pallas import tpu as pltpu
from jax.sharding import Mesh, PartitionSpec as P

D = 1024
HD = 64
SEQ = 1025
EPSILON = 1e-06
MASKED = -1000000000.0

HALF = 129
ROWS = 136
SLOTS = 8
NY = 4
NZ = 4

F32 = jnp.float32
BF = jnp.bfloat16
GROUP = ("xh", "y", "c")


def is_home(r, y):
    return y // 2 == r


def group_index(r, y, c):
    return (r * NY + y % NY) * 2 + c


def entry_pairs():
    places = [(r, y, c) for r in range(2) for y in range(NY) for c in range(2)]
    first, second = [], []
    for r, y, c in places:
        me = group_index(r, y, c)
        if is_home(r, y):
            first.append((me, group_index(r, y + 2, c)))
        else:
            first.append((me, group_index(1 - r, y, c)))
            second.append((me, group_index(1 - r, y + 2, c)))
    return first, second


ENTRY_FIRST, ENTRY_SECOND = entry_pairs()
EXIT_FIRST = [(b, a) for a, b in ENTRY_FIRST]
EXIT_SECOND = [(b, a) for a, b in ENTRY_SECOND]


def swap(value, axis):
    return lax.ppermute(value, axis, [(0, 1), (1, 0)])


def pull(value, axis, distance):
    return lax.ppermute(value, axis, [((i + distance) % 4, i) for i in range(4)])


def after(value, *earlier):
    return lax.optimization_barrier((value,) + earlier)[0]


def place_in(block, spare, home):
    first = jnp.concatenate([block[:HALF], spare], axis=0)
    second = jnp.concatenate([block[HALF:], spare], axis=0)
    moved = lax.ppermute(jnp.where(home, second, first), GROUP, ENTRY_FIRST)
    crossed = lax.ppermute(second, GROUP, ENTRY_SECOND)
    return jnp.where(home, first, moved), jnp.where(home, moved, crossed)


def place_out(values, home):
    own, other = values[:HALF, : D // 2], values[:HALF, D // 2 :].astype(BF)
    moved = lax.ppermute(jnp.where(home, other, own.astype(BF)), GROUP, EXIT_FIRST)
    crossed = lax.ppermute(other, GROUP, EXIT_SECOND)
    moved, crossed = moved.astype(F32), crossed.astype(F32)
    return jnp.concatenate([jnp.where(home, own, moved), jnp.where(home, moved, crossed)], axis=0)


def gather(piece, *beside):
    near = jnp.concatenate([piece] + [pull(piece, "y", d) for d in (1, 2, 3)], axis=0)
    near = after(near, *beside)
    return near, swap(near, "c")


def scatter_begin(halves, weight, contract, extra=None):
    def product(half):
        result = dot(half, weight, contract)
        if extra is not None:
            row = jnp.arange(NY * ROWS)[:, None] % ROWS - HALF
            for i in range(extra.shape[0]):
                result = jnp.where(row == i, extra[i], result)
        return result

    near, far = halves
    far = swap(product(far).astype(BF), "c")
    summed = product(near) + far.astype(F32)
    return summed[:ROWS], [summed[d * ROWS : (d + 1) * ROWS].astype(BF) for d in (1, 2, 3)]


def scatter_end(total, pieces):
    for d, piece in zip((1, 2, 3), pieces):
        total = total + pull(piece, "y", -d).astype(F32)
    return total


def image_sum(own, other):
    return own + swap(other.astype(BF), "xh").astype(F32)


def replica_scatter(arrays):
    z = lax.axis_index("z")

    def chunk(d):
        sizes = [values.shape[0] // NZ for values in arrays]
        cuts = [
            lax.dynamic_slice_in_dim(values, ((z + d) % NZ) * rows, rows, 0)
            for values, rows in zip(arrays, sizes)
        ]
        return jnp.concatenate(cuts, axis=0)

    total = chunk(0)
    for d in (1, 2, 3):
        total = total + pull(chunk(d).astype(BF), "z", -d).astype(F32)
    return total.astype(BF)


def replica_gather(total, split, *beside):
    z = lax.axis_index("z")
    total = (total.astype(F32) + swap(total, "xl").astype(F32)).astype(BF)
    total = after(total, *beside)
    pieces = [total] + [pull(total, "z", d) for d in (1, 2, 3)]

    def whole(parts):
        slots = []
        for k in range(NZ):
            d = (k - z) % NZ
            low = jnp.where(d == 0, parts[0], parts[1])
            high = jnp.where(d == 2, parts[2], parts[3])
            slots.append(jnp.where(d < 2, low, high).astype(F32))
        return jnp.concatenate(slots, axis=0)

    return whole([piece[:split] for piece in pieces]), whole([piece[split:] for piece in pieces])


def dot(first, second, contract):
    return lax.dot_general(
        first, second, (((contract[0],), (contract[1],)), ((), ())), preferred_element_type=F32
    )


def norm(values, gain, shift):
    center = jnp.mean(values, axis=1, keepdims=True)
    moved = values - center
    inverse = lax.rsqrt(jnp.mean(moved * moved, axis=1, keepdims=True) + EPSILON)
    scaled = moved * inverse
    return (scaled * gain + shift).astype(BF), scaled, inverse


def norm_pull(grad, scaled, inverse, gain):
    weighted = grad * gain
    mean = jnp.mean(weighted, axis=1, keepdims=True)
    inner = jnp.mean(weighted * scaled, axis=1, keepdims=True)
    return inverse * (weighted - mean - scaled * inner)


BLOCK = 272


def chances(query, key, mask):
    scores = dot(query * (1.0 / math.sqrt(HD)), key, (1, 1))
    scores = jnp.where(mask > 0, scores, MASKED)
    weights = jnp.exp(scores - jnp.max(scores, axis=1, keepdims=True))
    return weights * (1.0 / jnp.sum(weights, axis=1, keepdims=True))


def attend_kernel(mask_ref, packed_ref, out_ref):
    mask = mask_ref[...]
    for head in range(2):
        part = [slice(128 * s + HD * head, 128 * s + HD * (head + 1)) for s in range(3)]
        key, value = packed_ref[:, part[1]], packed_ref[:, part[2]]
        for block in range(SLOTS * ROWS // BLOCK):
            rows = slice(block * BLOCK, (block + 1) * BLOCK)
            chance = chances(packed_ref[rows, part[0]], key, mask).astype(BF)
            out_ref[rows, part[0]] = dot(chance, value, (1, 0)).astype(BF)


def attend_pull_kernel(mask_ref, packed_ref, grad_ref, out_ref):
    mask = mask_ref[...]
    factor = 1.0 / math.sqrt(HD)
    for head in range(2):
        part = [slice(128 * s + HD * head, 128 * s + HD * (head + 1)) for s in range(3)]
        key, value = packed_ref[:, part[1]], packed_ref[:, part[2]]
        key_grad = jnp.zeros((SLOTS * ROWS, HD), F32)
        value_grad = jnp.zeros((SLOTS * ROWS, HD), F32)
        for block in range(SLOTS * ROWS // BLOCK):
            rows = slice(block * BLOCK, (block + 1) * BLOCK)
            query, grad = packed_ref[rows, part[0]], grad_ref[rows, part[0]]
            chance = chances(query, key, mask)
            chance_grad = dot(grad, value, (1, 1))
            inner = jnp.sum(chance_grad * chance, axis=1, keepdims=True)
            score_grad = (chance * (chance_grad - inner)).astype(BF)
            out_ref[rows, part[0]] = (dot(score_grad, key, (1, 0)) * factor).astype(BF)
            key_grad = key_grad + dot(score_grad, query, (0, 0))
            value_grad = value_grad + dot(chance.astype(BF), grad, (0, 0))
        out_ref[:, part[1]] = (key_grad * factor).astype(BF)
        out_ref[:, part[2]] = value_grad.astype(BF)


def local_kernel(kernel, width, micros, *operands):
    return pl.pallas_call(
        kernel,
        out_shape=jax.ShapeDtypeStruct((SLOTS * ROWS, width), BF),
        in_specs=[pl.BlockSpec(memory_space=pltpu.VMEM)] * len(operands),
        out_specs=pl.BlockSpec(memory_space=pltpu.VMEM),
        compiler_params=pltpu.CompilerParams(vmem_limit_bytes=32 * 1024 * 1024),
        cost_estimate=pl.CostEstimate(
            flops=micros * 1000000000, bytes_accessed=micros * 3000000, transcendentals=0
        ),
    )(*operands)


def attend(packed, mask):
    return local_kernel(attend_kernel, 2 * HD, 8, mask, packed)


def attend_pull(packed, mask, mixture_grad):
    return local_kernel(attend_pull_kernel, 6 * HD, 12, mask, packed, mixture_grad)


def shards(
    inputs,
    w_qkv,
    qv_bias,
    w_out,
    w_fc1,
    fc1_bias,
    w_fc2,
    ln_gain,
    ln_bias,
    layer_scale,
    branch_bias,
    cotangent,
):
    r, y, c = (lax.axis_index(name) for name in GROUP)
    home = is_home(r, y)

    def in_order(mine, other):
        return jnp.where(r == 0, jnp.concatenate([mine, other]), jnp.concatenate([other, mine]))

    def pick(pair):
        return jnp.where(r == 0, pair[0], pair[1]), jnp.where(r == 0, pair[1], pair[0])

    own_rows = [ln_gain[0], ln_bias[0], layer_scale[0], branch_bias[0]]
    own_rows = jnp.concatenate(own_rows, axis=0)
    small = jnp.concatenate([qv_bias.reshape(-1), fc1_bias.reshape(-1)])
    spare = ROWS - HALF
    real = jnp.arange(ROWS)[:, None] < HALF
    mine, theirs = place_in(inputs, own_rows[:spare], home)
    x = jnp.where(real, jnp.concatenate([mine, theirs], axis=1).astype(F32), 0.0)
    rows = jnp.concatenate([own_rows[:spare], theirs[HALF:]], axis=1).astype(F32)
    gains, shifts, scales, first_bias = rows[0:2], rows[2:4], rows[4:6], rows[6:7]
    normed, scaled_first, inverse_first = norm(x, gains[0], shifts[0])
    normed_first = gather(normed)
    spare_rows = jnp.pad(own_rows[spare:], ((0, spare - 1), (0, 0)))
    mine, theirs = place_in(after(cotangent, normed_first[0]), spare_rows, home)
    upstream = jnp.where(real, jnp.concatenate([mine, theirs], axis=1).astype(F32), 0.0)
    second_bias = theirs[HALF : HALF + 1]
    second_bias = jnp.concatenate([own_rows[spare:], second_bias], axis=1).astype(F32)

    out_columns = w_out[0].reshape(128, 4, 128).transpose(1, 0, 2).reshape(D // 2, 128)
    first_weights = jnp.concatenate([w_qkv[0], out_columns], axis=1)
    small_row = jnp.pad(small[None], ((0, 15), (0, 128)))
    first_weights = jnp.concatenate([first_weights, small_row], axis=0)
    first_weights = swap(after(first_weights, normed), "xh")
    small_other = first_weights[D // 2, :384]
    qkv_weight = jnp.concatenate([w_qkv[0], first_weights[: D // 2, :384]], axis=0)
    qkv_weight = qkv_weight.reshape(D, 2, 3, HD).transpose(0, 2, 1, 3).reshape(D, 6 * HD)
    out_other = first_weights[: D // 2, 384:].reshape(4, 128, 128).transpose(1, 0, 2)
    out_block = jnp.concatenate([w_out[0], out_other.reshape(128, D // 2)], axis=1)
    fc1_other = swap(after(w_fc1[0], first_weights), "xh")
    fc2_other = swap(after(w_fc2[0], fc1_other), "xh")
    fc1_weight = jnp.concatenate([w_fc1[0], fc1_other], axis=0)
    fc2_weight = jnp.concatenate([w_fc2[0], fc2_other], axis=1)
    head_bias = in_order(small[:128], small_other[:128]).astype(F32).reshape(2, 2, HD)
    zeros = jnp.zeros((128,), F32)
    full_bias = jnp.concatenate([head_bias[:, 0].reshape(-1), zeros, head_bias[:, 1].reshape(-1)])
    unit_bias = in_order(small[128:], small_other[128:]).astype(F32)

    packed = [(dot(half, qkv_weight, (1, 0)) + full_bias).astype(BF) for half in normed_first]
    packed = jnp.concatenate(packed, axis=0)
    position = jnp.arange(SLOTS * ROWS)
    slot, local = position // ROWS, position % ROWS
    owner_y, owner_c = (y + slot % NY) % NY, c ^ (slot // NY)
    last = (owner_y == (2 * r + 3) % NY) & (owner_c == 1)
    mask = local < jnp.where(last, HALF - (8 * HALF - SEQ), HALF)
    mask = mask.astype(F32)[None]
    last_grad = (upstream * scales[1]).astype(BF)
    last_full = gather(after(last_grad, normed_first[0]))
    mixture = attend(after(packed, fc1_other, last_full[0]), mask)
    half_rows = NY * ROWS
    mixture_halves = mixture[:half_rows], mixture[half_rows:]
    begun, sent = scatter_begin(mixture_halves, out_block, (1, 0))
    branch_first = scatter_end(begun, sent) + first_bias
    x = x + scales[0] * branch_first

    normed, scaled_second, inverse_second = norm(x, gains[1], shifts[1])
    normed_second = gather(after(normed, fc2_other, last_full[1]))
    active, hidden_grad = [], []
    for half, grad in zip(normed_second, last_full):
        hidden = dot(half, fc1_weight, (1, 0)) + unit_bias
        spread = 0.5 * (1.0 + lax.erf(hidden * (1.0 / math.sqrt(2.0))))
        active.append((hidden * spread).astype(BF))
        slope = jnp.exp(-0.5 * hidden * hidden) * (1.0 / math.sqrt(2.0 * math.pi))
        slope = spread + hidden * slope
        hidden_grad.append((dot(grad, fc2_weight, (1, 1)) * slope).astype(BF))
    begun, sent = scatter_begin(hidden_grad, fc1_weight, (1, 1))
    normed_grad = scatter_end(begun, sent)
    fc2_grad = sum(dot(one, two, (0, 0)) for one, two in zip(active, last_full))
    fc1_grad = sum(dot(one, two, (0, 0)) for one, two in zip(normed_second, hidden_grad))
    unit_grad = sum(jnp.sum(half.astype(F32), axis=0) for half in hidden_grad)
    fc2_sum = image_sum(fc2_grad[:, : D // 2], after(fc2_grad[:, D // 2 :].astype(BF), *sent))
    fc1_sum = image_sum(fc1_grad[: D // 2], after(fc1_grad[D // 2 :].astype(BF), fc2_sum))
    scale_second = jnp.sum(fc2_weight.astype(F32) * fc2_grad, axis=0) / scales[1]
    scale_second = scale_second + second_bias[0] * jnp.sum(upstream, axis=0)

    upstream = upstream + norm_pull(normed_grad, scaled_second, inverse_second, gains[1])
    first_grad = after((upstream * scales[0]).astype(BF), fc2_sum)
    vectors = [
        jnp.sum(normed_grad * scaled_second, axis=0),
        jnp.sum(normed_grad, axis=0),
        jnp.sum(upstream * branch_first, axis=0),
        scale_second,
    ]
    carried = jnp.concatenate([first_grad[:HALF], jnp.stack(vectors).astype(BF)], axis=0)
    carried = gather(jnp.pad(carried, ((0, spare - 4), (0, 0))), fc1_sum)
    real = jnp.arange(NY * ROWS)[:, None] % ROWS < HALF
    first_full = [jnp.where(real, half, jnp.zeros((), BF)) for half in carried]
    spares = [half.reshape(NY, ROWS, D)[:, HALF : HALF + 4].astype(F32) for half in carried]
    vectors = sum(jnp.sum(half, axis=0) for half in spares)
    bias_first = sum(jnp.sum(half.astype(F32), axis=0, keepdims=True) for half in first_full)
    bias_second = sum(jnp.sum(half.astype(F32), axis=0, keepdims=True) for half in last_full)
    vectors = jnp.concatenate([vectors, bias_first, bias_second], axis=0)

    mixture_grad = [dot(half, out_block, (1, 1)).astype(BF) for half in first_full]
    fc_sum = jnp.concatenate([fc1_sum, fc2_sum], axis=0)
    mixture_grad = jnp.concatenate(mixture_grad, axis=0)
    out_grad = sum(dot(one, two, (0, 0)) for one, two in zip(first_full, mixture_halves))
    packed_grad = attend_pull(packed, mask, mixture_grad)
    packed_halves = packed_grad[:half_rows], packed_grad[half_rows:]
    qkv_grad = sum(dot(one, two, (0, 0)) for one, two in zip(normed_first, packed_halves))
    totals = jnp.sum(packed_grad.astype(F32), axis=0)
    wide_weight = qkv_weight.astype(F32)
    shift_part = jnp.sum(wide_weight * totals, axis=1)
    product = jnp.sum(wide_weight * qkv_grad, axis=1)
    gain_part = (product - shifts[0] * shift_part) / gains[0]
    late = jnp.concatenate([qkv_grad, out_grad], axis=1)
    head_grad = totals.reshape(3, 2, HD)
    head_grad = jnp.stack([head_grad[0], head_grad[2]], axis=1).reshape(2, 128)
    head_own, head_other = pick(head_grad)
    unit_own, unit_other = pick(unit_grad.reshape(2, 256))
    zeros = jnp.zeros((128,), F32)
    own = jnp.concatenate([unit_own, head_own, zeros])[None]
    other = jnp.concatenate([unit_other, head_other, zeros])[None]
    late_own = jnp.concatenate([late[: D // 2], vectors[:, : D // 2], own], axis=0)
    late_other = jnp.concatenate([late[D // 2 :], vectors[:, D // 2 :], other], axis=0)
    late_other = late_other.astype(BF)
    late = image_sum(late_own, late_other)

    final = jnp.stack([gain_part, shift_part])
    packed_halves = after(packed_halves, late_other)
    begun, sent = scatter_begin(packed_halves, qkv_weight, (1, 1), final)
    normed_grad = scatter_end(begun, sent)
    final = normed_grad[HALF : HALF + 2]
    final = final[:, : D // 2] + swap(final[:, D // 2 :], "xh")
    late = jnp.concatenate([late, final, jnp.zeros((32 - 9, D // 2), F32)], axis=0)
    active = [after(half, normed_grad) for half in active]
    begun, sent = scatter_begin(active, fc2_weight, (1, 0))
    branch_second = scatter_end(begun, after(sent, late)) + second_bias
    output = place_out(x + scales[1] * branch_second, home)
    first_pull = norm_pull(normed_grad, scaled_first, inverse_first, gains[0])
    input_grad = place_out(upstream + first_pull, home)
    quarter = replica_scatter([fc_sum, late])
    fc_sum, late = replica_gather(quarter, fc_sum.shape[0] // NZ, branch_second, first_pull)

    qkv_grad = late[: D // 2, :384].reshape(D // 2, 3, 2, HD).transpose(0, 2, 1, 3)
    out_grad = late[: D // 2, 384:].T
    vectors, final = late[D // 2 : D // 2 + 7], late[D // 2 + 7 : D // 2 + 9]
    small = vectors[6]
    return (
        output,
        input_grad,
        qkv_grad.reshape(1, D // 2, 384),
        small[256:384].reshape(1, 1, 1, 1, -1),
        out_grad[None],
        fc_sum[None, : D // 2],
        small[:256].reshape(1, 1, 1, -1),
        fc_sum[None, D // 2 :],
        jnp.stack([final[0], vectors[0]])[None],
        jnp.stack([final[1], vectors[1]])[None],
        vectors[2:4][None],
        vectors[4:6][None],
    )


def solution(mesh):
    fine = Mesh(mesh.devices.reshape(NZ, 2, 2, NY, 2), ("z", "xl") + GROUP)
    tokens = P(("z", "xl", "y", "c"), "xh")
    tall = P(None, "xh", ("y", "c"))
    wide = P(None, ("y", "c"), "xh")
    head = P(None, ("y", "c"), "xh", None, None)
    unit = P(None, ("y", "c"), "xh", None)
    vector = P(None, None, "xh")
    return jax.shard_map(
        shards,
        mesh=fine,
        in_specs=(
            tokens,
            tall,
            head,
            wide,
            tall,
            unit,
            wide,
            vector,
            vector,
            vector,
            vector,
            tokens,
        ),
        out_specs=(
            tokens,
            tokens,
            tall,
            head,
            wide,
            tall,
            unit,
            wide,
            vector,
            vector,
            vector,
            vector,
        ),
        check_vma=False,
    )
```
